256 devices in a mesh: ctx: 16 (over x_hi, y, core), exp: 16 (over z, x_lo).
Axes of the slice: x: 4 (x_hi: 2, x_lo: 2; x = x_hi * 2 + x_lo), y: 4, z: 8, core: 2. Of those that a mesh axis runs over, the one named last changes fastest.
Arguments:
- layer_input: bfloat16 [16, 2048, 2048], P('exp', 'ctx'), may hold values from -6 to 6
- queries: bfloat16 [16, 2048, 1024], P('exp', 'ctx'), may hold values from -5 to 5
- keys: bfloat16 [16, 2048, 1024], P('exp', 'ctx'), may hold values from -5 to 5
- values: bfloat16 [16, 2048, 1024], P('exp', 'ctx'), may hold values from -6 to 6
- out_weight: bfloat16 [1024, 2048], replicated, may hold values from -0.1875 to 0.1875
- norm_gain: float32 [2048], replicated, may hold values from 0.1 to 1.9
- route_ids: int32 [16, 2048, 6], P('exp', 'ctx'), may hold values from 0 to 31, all different within a row; in each aligned block of 128 rows (0 to 127, 128 to 255, ..., all dimensions but the last counted through in order) at most 28 rows name the same one
- route_weight: float32 [16, 2048, 6], P('exp', 'ctx'), may hold values from 0.05 to 0.4
- w_gate: bfloat16 [32, 2048, 704], P('exp', 'ctx'), may hold values from -0.125 to 0.125
- w_up: bfloat16 [32, 2048, 704], P('exp', 'ctx'), may hold values from -0.125 to 0.125
- w_down: bfloat16 [32, 704, 2048], P('exp', None, 'ctx'), may hold values from -0.21875 to 0.21875
Outputs:
- mixed: bfloat16 [16, 2048, 2048], P('exp', 'ctx')
The draws below stay inside these ranges and needn't reach their ends.
Inputs may be any that keep to these rules, and one draw needn't show every extreme that they name: `route_ids`: each token names 6 different experts; among the 128 tokens of one device no expert is named more than 28 times, and on some device one expert is named exactly 28 times.
All inputs are finite; a program needn't handle non-finite values.
Results may differ from the reference program's by a relative error of at most 0.015.
Values may be sent and summed in bfloat16 or wider, within the bound.
No kernel may reach another device: no remote copies, remote signals or barrier semaphores. Data moves between devices by JAX's collectives and lax.ppermute only.
A program may use at most 128 MiB of HBM per device.

```python
import math
import jax
import jax.numpy as jnp
import numpy as np
from jax import lax

D = 2048
HEADS = 8
HD = 128
EXPERTS = 32
FFE = 704
TOP = 6
TOK_DEV = 128
CAP = 28
SEQS = 16
LEN = 2048
N_CTX = 16
N_EXP = 16


def drawn_pair(key):
    shape = (SEQS, LEN, HEADS * HD)
    first = jnp.clip(jax.random.normal(jax.random.fold_in(key, 101), shape, jnp.float32) * 1.6, -5.0, 5.0)
    second = jnp.clip(jax.random.normal(jax.random.fold_in(key, 202), shape, jnp.float32) * 1.6, -5.0, 5.0)
    return (first, second)


def draw_queries(key, part):
    both = drawn_pair(key)
    return both[0].astype(jnp.bfloat16)


def draw_keys(key, part):
    both = drawn_pair(key)
    return both[1].astype(jnp.bfloat16)


def block_levels(own_key, shape, shards, low, high):
    loudness = 1.0
    for axis_at, parts in shards:
        draws = jax.random.uniform(jax.random.fold_in(jax.random.fold_in(own_key, 6), axis_at), (parts,), jnp.float32, low / len(shards), high / len(shards))
        loudness = loudness * jnp.repeat(jnp.exp(draws), shape[axis_at] // parts).reshape((-1,) + (1,) * (len(shape) - 1 - axis_at))
    return loudness


def shared_out(stream_key, own, number, rows, count, top, limit, skew):
    ranking = jax.random.permutation(stream_key, count)
    crowded, usual = load_shares(count, rows * top, limit, skew, True), load_shares(count, rows * top, limit, skew, False)
    places = jnp.arange(count)

    def named(sizes, turn):
        used = int((sizes > 0).sum())
        fixed = max(1, used // 4)
        shifted = fixed + (places - fixed + turn * (used - fixed)) % max(1, count - fixed)
        return jnp.zeros((count,), jnp.int32).at[ranking[jnp.where(places < fixed, places, shifted)]].set(jnp.asarray(sizes, jnp.int32))

    sizes = jnp.where(number % 4 == 0, named(crowded, number // 4), named(usual, number - number // 4 - 1))
    mixed = jax.random.permutation(jax.random.fold_in(own, 3), count)
    donor, receiver = mixed[0:count // 2 * 2:2], mixed[1:count // 2 * 2:2]
    slack = jnp.minimum(sizes[donor] - 1, limit - sizes[receiver]) // 2
    slack = jnp.where((donor == ranking[0]) | (receiver == ranking[0]) | (sizes[receiver] == 0), 0, jnp.maximum(slack, 0))
    shifted = jax.random.randint(jax.random.fold_in(own, 4), (count // 2,), 0, 1 << 20) % (slack + 1)
    sizes = sizes.at[donor].add(-shifted).at[receiver].add(shifted)
    labels = jnp.searchsorted(jnp.cumsum(sizes), jnp.arange(rows * top), side="right").astype(jnp.int32)
    table = labels.reshape(top, rows).T
    table = table[jax.random.permutation(jax.random.fold_in(own, 1), rows)]
    turn = jax.random.randint(jax.random.fold_in(own, 2), (rows, 1), 0, top)
    return jnp.take_along_axis(table, (jnp.arange(top)[None, :] + turn) % top, axis=1)


def load_shares(amount, total, reach, skew, full):
    loads = [(1 << 20) // math.isqrt(standing ** skew) + 1 for standing in range(1, amount + 1)]
    largest = reach if full else min(reach, max(-(-total // amount), total * loads[0] // sum(loads)))
    least = 1 if total - largest >= amount - 1 else 0
    counts, rest = [largest] + [least] * (amount - 1), total - largest - least * (amount - 1)
    while rest > 0:
        candidates = [i for i in range(1, amount) if counts[i] < largest] or [i for i in range(1, amount) if counts[i] < reach]
        pool, remaining = sum([loads[i] for i in candidates]), rest
        for i in candidates:
            more = min(reach - counts[i], max(1, remaining * loads[i] // pool), rest)
            counts[i] = counts[i] + more
            rest = rest - more
    return np.array(counts)


def scatter_about(key, extent, scale, most, split=(), held_as=jnp.bfloat16):
    values = scale * jax.random.normal(key, extent, jnp.float32)
    if split:
        values = values * block_levels(key, extent, split, -0.22, 0.18)
    return jnp.clip(values, -most, most).astype(held_as)


def setup_inputs(seed: int = 0) -> dict:
    seeds = jax.random.split(jax.random.key(seed), 12)
    layer_input = scatter_about(seeds[0], (SEQS, LEN, D), 1.0, 6.0, ((0, 16), (1, 16)))
    queries = draw_queries(jax.random.fold_in(seeds[11], 71), 0)
    keys = draw_keys(jax.random.fold_in(seeds[11], 71), 0)
    values = scatter_about(seeds[3], (SEQS, LEN, HEADS * HD), 1.0, 6.0, ((0, 16), (1, 16)))
    out_weight = scatter_about(seeds[4], (HEADS * HD, D), (HEADS * HD) ** -0.5, 0.1875)
    norm_gain = jnp.clip(1.0 + 0.18 * jax.random.normal(seeds[5], (D,), jnp.float32), 0.1, 1.9)
    route_ids_keys = jax.random.split(jax.random.fold_in(seeds[6], 1), SEQS * LEN // TOK_DEV)
    route_ids_turns = jax.random.permutation(jax.random.fold_in(seeds[6], 3), SEQS * LEN // TOK_DEV)
    route_ids = jax.vmap(lambda own, number: shared_out(jax.random.fold_in(seeds[6], 2), own, number, TOK_DEV, EXPERTS, TOP, CAP, 1))(route_ids_keys, route_ids_turns).reshape((SEQS, LEN, TOP))
    route_weight = jnp.clip(0.05 + 0.35 * jax.random.uniform(seeds[7], (SEQS, LEN, TOP), jnp.float32) ** block_levels(seeds[7], (SEQS, LEN, TOP), ((0, 16), (1, 16)), -0.2, 0.2), 0.05, 0.4)
    w_gate = scatter_about(seeds[8], (EXPERTS, D, FFE), D ** -0.5, 0.125, ((0, 16), (1, 16)))
    w_up = scatter_about(seeds[9], (EXPERTS, D, FFE), D ** -0.5, 0.125, ((0, 16), (1, 16)))
    w_down = scatter_about(seeds[10], (EXPERTS, FFE, D), FFE ** -0.5, 0.21875, ((0, 16), (2, 16)))
    return {"layer_input": layer_input, "queries": queries, "keys": keys, "values": values, "out_weight": out_weight, "norm_gain": norm_gain, "route_ids": route_ids, "route_weight": route_weight, "w_gate": w_gate, "w_up": w_up, "w_down": w_down}


def attend(triple):
    query_seq, key_seq, value_seq = triple
    length = query_seq.shape[0]
    query_f = query_seq.astype(jnp.float32).reshape(length, HEADS, HD)
    key_f = key_seq.astype(jnp.float32).reshape(length, HEADS, HD)
    value_f = value_seq.astype(jnp.float32).reshape(length, HEADS, HD)
    scores = jnp.einsum('qhd,khd->hqk', query_f, key_f, precision=lax.Precision.HIGHEST) / math.sqrt(HD)
    allowed = (jnp.arange(length)[:, None] >= jnp.arange(length)[None, :])[None]
    masked = jnp.where(allowed, scores, -1e+30)
    row_max = lax.optimization_barrier(jnp.max(masked, axis=-1, keepdims=True))
    probs = jnp.where(allowed, jnp.exp(masked - row_max), 0.0)
    total = lax.optimization_barrier(jnp.sum(probs, axis=-1))
    probs_b = probs.astype(jnp.bfloat16).astype(jnp.float32)
    heads_out = jnp.einsum('hqk,khd->hqd', probs_b, value_f, precision=lax.Precision.HIGHEST) / total[..., None]
    return heads_out.transpose(1, 0, 2).reshape(length, HEADS * HD).astype(jnp.bfloat16)

def reference(layer_input, queries, keys, values, out_weight, norm_gain, route_ids, route_weight, w_gate, w_up, w_down):
    attended = lax.map(attend, (queries, keys, values))
    total = SEQS * LEN
    flat_att = attended.reshape(total, HEADS * HD)
    residual = (layer_input.reshape(total, D).astype(jnp.float32) + jnp.dot(flat_att, out_weight, preferred_element_type=jnp.float32)).astype(jnp.bfloat16)
    res_f = residual.astype(jnp.float32)
    normed = (res_f * lax.rsqrt(lax.optimization_barrier(jnp.mean(res_f * res_f, axis=-1, keepdims=True)) + 1e-06) * norm_gain).astype(jnp.bfloat16)
    picks = route_ids.reshape(-1).astype(jnp.int32)
    pick_weight = route_weight.reshape(-1)
    bound = N_CTX * N_EXP * CAP

    def per_expert(accum, expert):
        chosen = picks == expert
        found = jnp.nonzero(chosen, size=bound, fill_value=0)[0].astype(jnp.int32)
        live = (jnp.arange(bound) < jnp.sum(chosen.astype(jnp.int32))).astype(jnp.float32)
        token_index = (found // TOP).astype(jnp.int32)
        rows = normed[token_index]
        gate_val = jnp.dot(rows, w_gate[expert], preferred_element_type=jnp.float32)
        up_val = jnp.dot(rows, w_up[expert], preferred_element_type=jnp.float32)
        hidden = (jax.nn.silu(gate_val) * up_val).astype(jnp.bfloat16)
        expert_out = jnp.dot(hidden, w_down[expert], preferred_element_type=jnp.float32).astype(jnp.bfloat16)
        scaled = expert_out.astype(jnp.float32) * (pick_weight[found] * live)[:, None]
        return (accum.at[token_index].add(scaled), None)
    accum, _ = lax.scan(per_expert, jnp.zeros((total, D), jnp.float32), jnp.arange(EXPERTS, dtype=jnp.int32))
    mixed = (res_f + accum).astype(jnp.bfloat16)
    return mixed.reshape(SEQS, LEN, D)
```

```python
import functools
import math

import jax
import jax.numpy as jnp
from jax import lax
from jax.experimental import pallas as pl
from jax.experimental.pallas import tpu as pltpu
from jax.sharding import PartitionSpec as P

HD = 128
SLOT = 32
NY = 4
NZ = 8
BATCHES = ((0,), (1, 7), (2, 6), (3, 5), (4,))


def ctx_pairs(dx, dy, dc):
    pairs = []
    for i in range(16):
        xh, y, c = i // 8, i // 2 % NY, i % 2
        pairs.append((i, ((xh + dx) % 2 * NY + (y + dy) % NY) * 2 + (c + dc) % 2))
    return pairs


def z_pairs(d):
    return [(z * 2 + x, (z + d) % NZ * 2 + x) for z in range(NZ) for x in range(2)]


def ctx_shift(a, dx, dy, dc):
    return lax.ppermute(a, "ctx", ctx_pairs(dx, dy, dc))


def z_shift(a, d):
    return lax.ppermute(a, "exp", z_pairs(d))


def x_swap(a):
    return lax.ppermute(a, "exp", [(i, i ^ 1) for i in range(16)])


def diag_swap(a):
    pairs = [(c * 16 + e, (c ^ 1) * 16 + (e ^ 1)) for c in range(16) for e in range(16)]
    return lax.ppermute(a, ("ctx", "exp"), pairs)


def attend_kernel(core_ref, own_ref, other_ref, out_ref):
    count = own_ref.shape[0]
    core = core_ref[0]
    row = lax.broadcasted_iota(jnp.int32, (HD, HD), 0)
    col = lax.broadcasted_iota(jnp.int32, (HD, HD), 1)
    dims = (((1,), (1,)), ((), ()))
    scale = 1.0 / math.sqrt(HD)
    for p in range(count):
        q = own_ref[p, 0]
        width = (p + 1) * HD
        k_own = own_ref[: p + 1, 1].reshape(width, HD)
        v_own = own_ref[: p + 1, 2].reshape(width, HD)
        k_oth = other_ref[: p + 1, 0].reshape(width, HD)
        v_oth = other_ref[: p + 1, 1].reshape(width, HD)
        s_own = lax.dot_general(q, k_own, dims, preferred_element_type=jnp.float32) * scale
        s_oth = lax.dot_general(q, k_oth, dims, preferred_element_type=jnp.float32) * scale
        last_own = jnp.where(row >= col, s_own[:, p * HD :], -1e30)
        last_oth = jnp.where(core == 1, s_oth[:, p * HD :], -1e30)
        if p:
            s_own = jnp.concatenate([s_own[:, : p * HD], last_own], axis=1)
            s_oth = jnp.concatenate([s_oth[:, : p * HD], last_oth], axis=1)
        else:
            s_own, s_oth = last_own, last_oth
        top = jnp.maximum(
            jnp.max(s_own, axis=-1, keepdims=True), jnp.max(s_oth, axis=-1, keepdims=True)
        )
        e_own = jnp.exp(s_own - top)
        e_oth = jnp.exp(s_oth - top)
        total = jnp.sum(e_own, axis=-1, keepdims=True) + jnp.sum(e_oth, axis=-1, keepdims=True)
        acc = jnp.dot(e_own.astype(jnp.bfloat16), v_own, preferred_element_type=jnp.float32)
        acc += jnp.dot(e_oth.astype(jnp.bfloat16), v_oth, preferred_element_type=jnp.float32)
        out_ref[p] = (acc / total).astype(jnp.bfloat16)


def attend(core, own, other):
    count = own.shape[0]
    return pl.pallas_call(
        attend_kernel,
        out_shape=jax.ShapeDtypeStruct((count, HD, HD), jnp.bfloat16),
        in_specs=[
            pl.BlockSpec(memory_space=pltpu.SMEM),
            pl.BlockSpec(memory_space=pltpu.VMEM),
            pl.BlockSpec(memory_space=pltpu.VMEM),
        ],
        out_specs=pl.BlockSpec(memory_space=pltpu.VMEM),
        compiler_params=pltpu.CompilerParams(vmem_limit_bytes=32 * 2**20),
        cost_estimate=pl.CostEstimate(
            flops=700_000_000, bytes_accessed=1_600_000, transcendentals=1_200_000
        ),
    )(core, own, other)


def project_kernel(att_ref, weight_ref, input_ref, gain_ref, res_ref, normed_ref):
    heads = att_ref.shape[0]
    att = jnp.concatenate([att_ref[h] for h in range(heads)], axis=1)
    width = weight_ref.shape[1]
    tile = 512
    square = jnp.zeros((att.shape[0], 1), jnp.float32)
    for j in range(width // tile):
        cols = slice(j * tile, (j + 1) * tile)
        part = jnp.dot(att, weight_ref[:, cols], preferred_element_type=jnp.float32)
        part = (part + input_ref[:, cols].astype(jnp.float32)).astype(jnp.bfloat16)
        res_ref[:, cols] = part
        part = part.astype(jnp.float32)
        square += jnp.sum(part * part, axis=-1, keepdims=True)
    factor = lax.rsqrt(square / width + 1e-06)
    for j in range(width // tile):
        cols = slice(j * tile, (j + 1) * tile)
        normed_ref[:, cols] = (
            res_ref[:, cols].astype(jnp.float32) * factor * gain_ref[:, cols]
        ).astype(jnp.bfloat16)


def project(att, weight, layer_input, gain):
    shape = jax.ShapeDtypeStruct(layer_input.shape, jnp.bfloat16)
    return pl.pallas_call(
        project_kernel,
        out_shape=(shape, shape),
        in_specs=[pl.BlockSpec(memory_space=pltpu.VMEM)] * 4,
        out_specs=(pl.BlockSpec(memory_space=pltpu.VMEM),) * 2,
        compiler_params=pltpu.CompilerParams(vmem_limit_bytes=32 * 2**20),
        cost_estimate=pl.CostEstimate(
            flops=540_000_000, bytes_accessed=6_000_000, transcendentals=128
        ),
    )(att, weight, layer_input, gain)


def expert_kernel(pieces, x_ref, in_ref, down_ref, out_ref, acc_ref, hid_ref):
    step = pl.program_id(0)
    ffe = hid_ref.shape[1]

    @pl.when(step < pieces)
    def _():
        part = jnp.dot(x_ref[...], in_ref[0], preferred_element_type=jnp.float32)

        @pl.when(step == 0)
        def _():
            acc_ref[...] = part

        @pl.when(step > 0)
        def _():
            acc_ref[...] += part

    @pl.when(step == pieces - 1)
    def _():
        gate = acc_ref[:, :ffe]
        up = acc_ref[:, ffe:]
        hid_ref[...] = (gate / (1.0 + jnp.exp(-gate)) * up).astype(jnp.bfloat16)

    @pl.when(step >= pieces)
    def _():
        out_ref[...] = jnp.dot(
            hid_ref[...], down_ref[0], preferred_element_type=jnp.float32
        ).astype(jnp.bfloat16)


def expert(x, w_in, w_down):
    rows, width = x.shape
    pieces, depth, both = w_in.shape
    ffe = both // 2
    return pl.pallas_call(
        functools.partial(expert_kernel, pieces),
        grid=(2 * pieces,),
        out_shape=jax.ShapeDtypeStruct((rows, width), jnp.bfloat16),
        in_specs=[
            pl.BlockSpec((rows, depth), lambda i: (0, jnp.minimum(i, pieces - 1))),
            pl.BlockSpec((1, depth, both), lambda i: (jnp.minimum(i, pieces - 1), 0, 0)),
            pl.BlockSpec((1, ffe, depth), lambda i: (jnp.maximum(i - pieces, 0), 0, 0)),
        ],
        out_specs=pl.BlockSpec((rows, depth), lambda i: (0, jnp.maximum(i - pieces, 0))),
        scratch_shapes=[
            pltpu.VMEM((rows, both), jnp.float32),
            pltpu.VMEM((rows, ffe), jnp.bfloat16),
        ],
        compiler_params=pltpu.CompilerParams(vmem_limit_bytes=40 * 2**20),
        cost_estimate=pl.CostEstimate(
            flops=6 * rows * width * ffe,
            bytes_accessed=6 * width * ffe + 4 * rows * width,
            transcendentals=rows * ffe,
        ),
    )(x, w_in, w_down)


def gather_pieces(piece, xh, y):
    far = ctx_shift(piece, 1, 0, 0)
    near_up, near_down = ctx_shift(piece, 0, 1, 0), ctx_shift(piece, 0, -1, 0)
    far_up, far_down = ctx_shift(far, 0, 1, 0), ctx_shift(far, 0, -1, 0)
    near_two, far_two = ctx_shift(near_up, 0, 1, 0), ctx_shift(far_down, 0, -1, 0)
    out = jnp.zeros((2 * NY,) + piece.shape, piece.dtype)
    for dx, dy, part in (
        (0, 0, piece),
        (1, 0, far),
        (0, -1, near_up),
        (0, 1, near_down),
        (1, -1, far_up),
        (1, 1, far_down),
        (0, 2, near_two),
        (1, 2, far_two),
    ):
        place = (xh + dx) % 2 * NY + (y + dy) % NY
        out = lax.dynamic_update_slice(out, part[None], (place, 0, 0))
    return out


def body(
    layer_input,
    queries,
    keys,
    values,
    out_weight,
    norm_gain,
    route_ids,
    route_weight,
    w_gate,
    w_up,
    w_down,
):
    tok = layer_input.shape[1]
    ctx = lax.axis_index("ctx")
    exp = lax.axis_index("exp")
    core, y, xh = ctx % 2, ctx // 2 % NY, ctx // (2 * NY)
    z, xl = exp // 2, exp % 2
    same_core = [[p * 2 + c for p in range(2 * NY)] for c in range(2)]
    z_rings = [[i * 2 + x for i in range(NZ)] for x in range(2)]

    heads = jnp.stack([queries[0], keys[0], values[0]]).reshape(3, tok, -1, HD)
    heads = heads.transpose(2, 0, 1, 3)
    own = lax.all_to_all(heads, "ctx", 0, 0, axis_index_groups=same_core, tiled=True)
    other = ctx_shift(own[:, 1:], 0, 0, 1)
    attended = attend(core.reshape(1), own, other)
    attended = lax.all_to_all(attended, "ctx", 0, 0, axis_index_groups=same_core, tiled=True)

    def mine(w):
        return lax.dynamic_index_in_dim(w, core, 0, keepdims=False)

    def theirs(w):
        return lax.dynamic_index_in_dim(w, 1 - core, 0, keepdims=False)

    in_mine = jnp.concatenate([mine(w_gate), mine(w_up)], axis=1)
    in_come = ctx_shift(jnp.concatenate([theirs(w_gate), theirs(w_up)], axis=1), 0, 0, 1)
    down_mine = mine(w_down)
    down_come = ctx_shift(theirs(w_down), 0, 0, 1)
    first = core == 0
    in_piece = jnp.concatenate(
        [jnp.where(first, in_mine, in_come), jnp.where(first, in_come, in_mine)], axis=0
    )
    down_piece = jnp.concatenate(
        [jnp.where(first, down_mine, down_come), jnp.where(first, down_come, down_mine)], axis=1
    )
    w_in = gather_pieces(in_piece, xh, y)
    w_out = gather_pieces(down_piece, xh, y)

    picks = jnp.concatenate([route_ids[0].T.astype(jnp.float32), route_weight[0].T], axis=0)
    picks = lax.all_gather(picks, "exp", axis_index_groups=z_rings)
    picks = jnp.take(picks, (z - jnp.arange(NZ)) % NZ, axis=0)
    top = route_ids.shape[2]
    ids, weights = picks[:, :top], picks[:, top:]
    quarter = jnp.arange(4)
    wanted = (4 * z + ((2 * xl + core) ^ quarter)).astype(jnp.float32)
    hits = ids[:, None] == wanted[None, :, None, None]
    hit = jnp.sum(hits.astype(jnp.float32), axis=2)
    share = jnp.sum(jnp.where(hits, weights[:, None], 0.0), axis=2)
    before = (jnp.arange(tok)[:, None] < jnp.arange(tok)[None, :]).astype(jnp.bfloat16)
    rank = jnp.einsum(
        "drs,st->drt", hit.astype(jnp.bfloat16), before, preferred_element_type=jnp.float32
    )
    slots = jnp.arange(SLOT, dtype=jnp.float32)
    at_slot = rank[:, :, None, :] == slots[None, None, :, None]
    placing = jnp.where(at_slot, hit[:, :, None, :], 0.0).reshape(NZ, 4 * SLOT, tok)
    placing = placing.astype(jnp.bfloat16)
    merging = jnp.where(at_slot, share[:, :, None, :], 0.0).reshape(NZ, 4 * SLOT, tok)
    merging = merging.transpose(0, 2, 1).astype(jnp.bfloat16)

    residual, normed = project(attended, out_weight, layer_input[0], norm_gain[None])

    blocks = {0: normed}
    for d in (1, 2, 3):
        blocks[d] = z_shift(blocks[d - 1], 1)
        blocks[NZ - d] = z_shift(blocks[(NZ - d + 1) % NZ], -1)
    half = tok // 2
    blocks[4] = jnp.concatenate(
        [z_shift(blocks[3][:half], 1), z_shift(blocks[5][half:], -1)], axis=0
    )
    swaps = (lambda a: a, lambda a: ctx_shift(a, 0, 0, 1), x_swap, diag_swap)
    returned = {}
    for batch in BATCHES:
        rows = [
            jnp.dot(placing[d], blocks[d], preferred_element_type=jnp.float32).astype(
                jnp.bfloat16
            )
            for d in batch
        ]
        rows = jnp.stack(rows).reshape(len(batch), 4, SLOT, -1)
        arrived = jnp.stack([swaps[r](rows[:, r]) for r in range(4)])
        made = expert(arrived.reshape(-1, arrived.shape[-1]), w_in, w_out)
        made = made.reshape(arrived.shape)
        back = jnp.stack([swaps[r](made[r]) for r in range(4)], axis=1)
        for i, d in enumerate(batch):
            returned[d] = back[i].reshape(4 * SLOT, -1)

    def part(d):
        return jnp.dot(merging[d], returned[d], preferred_element_type=jnp.float32)

    def narrow(a):
        return a.astype(jnp.bfloat16)

    def wide(a):
        return a.astype(jnp.float32)

    farthest = narrow(part(4))
    up = z_shift(farthest[:half], 1)
    down = z_shift(farthest[half:], -1)
    pad = jnp.zeros_like(up)
    up = jnp.concatenate([up, pad], axis=0)
    down = jnp.concatenate([pad, down], axis=0)
    for d in (3, 2, 1):
        up = z_shift(narrow(part(NZ - d) + wide(up)), 1)
        down = z_shift(narrow(part(d) + wide(down)), -1)
    mixed = wide(residual) + part(0) + wide(up) + wide(down)
    return narrow(mixed)[None]


def solution(mesh):
    return jax.shard_map(
        body,
        mesh=mesh,
        in_specs=(
            P("exp", "ctx", None),
            P("exp", "ctx", None),
            P("exp", "ctx", None),
            P("exp", "ctx", None),
            P(),
            P(),
            P("exp", "ctx", None),
            P("exp", "ctx", None),
            P("exp", "ctx", None),
            P("exp", "ctx", None),
            P("exp", None, "ctx"),
        ),
        out_specs=P("exp", "ctx", None),
        check_vma=False,
    )
```

```python
import functools
import math

import jax
import jax.numpy as jnp
from jax import lax
from jax.experimental import pallas as pl
from jax.experimental.pallas import tpu as pltpu
from jax.sharding import PartitionSpec as P

HD = 128
SLOT = 32
NY = 4
NZ = 8
BATCHES = ((0, 1, 7, 2, 6), (3, 5), (4,))


def ctx_pairs(dx, dy, dc):
    pairs = []
    for i in range(16):
        xh, y, c = i // 8, i // 2 % NY, i % 2
        pairs.append((i, ((xh + dx) % 2 * NY + (y + dy) % NY) * 2 + (c + dc) % 2))
    return pairs


def z_pairs(d):
    return [(z * 2 + x, (z + d) % NZ * 2 + x) for z in range(NZ) for x in range(2)]


def ctx_shift(a, dx, dy, dc):
    return lax.ppermute(a, "ctx", ctx_pairs(dx, dy, dc))


def z_shift(a, d):
    return lax.ppermute(a, "exp", z_pairs(d))


def x_swap(a):
    return lax.ppermute(a, "exp", [(i, i ^ 1) for i in range(16)])


def diag_swap(a):
    pairs = [(c * 16 + e, (c ^ 1) * 16 + (e ^ 1)) for c in range(16) for e in range(16)]
    return lax.ppermute(a, ("ctx", "exp"), pairs)


def attend_kernel(core_ref, own_ref, other_ref, out_ref):
    count = own_ref.shape[0]
    core = core_ref[0]
    row = lax.broadcasted_iota(jnp.int32, (HD, HD), 0)
    col = lax.broadcasted_iota(jnp.int32, (HD, HD), 1)
    dims = (((1,), (1,)), ((), ()))
    scale = 1.0 / math.sqrt(HD)
    for p in range(count):
        q = own_ref[p, 0]
        width = (p + 1) * HD
        k_own = own_ref[: p + 1, 1].reshape(width, HD)
        v_own = own_ref[: p + 1, 2].reshape(width, HD)
        k_oth = other_ref[: p + 1, 0].reshape(width, HD)
        v_oth = other_ref[: p + 1, 1].reshape(width, HD)
        s_own = lax.dot_general(q, k_own, dims, preferred_element_type=jnp.float32) * scale
        s_oth = lax.dot_general(q, k_oth, dims, preferred_element_type=jnp.float32) * scale
        last_own = jnp.where(row >= col, s_own[:, p * HD :], -1e30)
        last_oth = jnp.where(core == 1, s_oth[:, p * HD :], -1e30)
        if p:
            s_own = jnp.concatenate([s_own[:, : p * HD], last_own], axis=1)
            s_oth = jnp.concatenate([s_oth[:, : p * HD], last_oth], axis=1)
        else:
            s_own, s_oth = last_own, last_oth
        top = jnp.maximum(
            jnp.max(s_own, axis=-1, keepdims=True), jnp.max(s_oth, axis=-1, keepdims=True)
        )
        e_own = jnp.exp(s_own - top)
        e_oth = jnp.exp(s_oth - top)
        total = jnp.sum(e_own, axis=-1, keepdims=True) + jnp.sum(e_oth, axis=-1, keepdims=True)
        acc = jnp.dot(e_own.astype(jnp.bfloat16), v_own, preferred_element_type=jnp.float32)
        acc += jnp.dot(e_oth.astype(jnp.bfloat16), v_oth, preferred_element_type=jnp.float32)
        out_ref[p] = (acc / total).astype(jnp.bfloat16)


def attend(core, own, other):
    count = own.shape[0]
    return pl.pallas_call(
        attend_kernel,
        out_shape=jax.ShapeDtypeStruct((count, HD, HD), jnp.bfloat16),
        in_specs=[
            pl.BlockSpec(memory_space=pltpu.SMEM),
            pl.BlockSpec(memory_space=pltpu.VMEM),
            pl.BlockSpec(memory_space=pltpu.VMEM),
        ],
        out_specs=pl.BlockSpec(memory_space=pltpu.VMEM),
        compiler_params=pltpu.CompilerParams(vmem_limit_bytes=32 * 2**20),
        cost_estimate=pl.CostEstimate(
            flops=700_000_000, bytes_accessed=1_600_000, transcendentals=1_200_000
        ),
    )(core, own, other)


def project_kernel(att_ref, weight_ref, input_ref, gain_ref, res_ref, normed_ref):
    heads = att_ref.shape[0]
    att = jnp.concatenate([att_ref[h] for h in range(heads)], axis=1)
    width = weight_ref.shape[1]
    tile = 512
    square = jnp.zeros((att.shape[0], 1), jnp.float32)
    for j in range(width // tile):
        cols = slice(j * tile, (j + 1) * tile)
        part = jnp.dot(att, weight_ref[:, cols], preferred_element_type=jnp.float32)
        part = (part + input_ref[:, cols].astype(jnp.float32)).astype(jnp.bfloat16)
        res_ref[:, cols] = part
        part = part.astype(jnp.float32)
        square += jnp.sum(part * part, axis=-1, keepdims=True)
    factor = lax.rsqrt(square / width + 1e-06)
    for j in range(width // tile):
        cols = slice(j * tile, (j + 1) * tile)
        normed_ref[:, cols] = (
            res_ref[:, cols].astype(jnp.float32) * factor * gain_ref[:, cols]
        ).astype(jnp.bfloat16)


def project(att, weight, layer_input, gain):
    shape = jax.ShapeDtypeStruct(layer_input.shape, jnp.bfloat16)
    return pl.pallas_call(
        project_kernel,
        out_shape=(shape, shape),
        in_specs=[pl.BlockSpec(memory_space=pltpu.VMEM)] * 4,
        out_specs=(pl.BlockSpec(memory_space=pltpu.VMEM),) * 2,
        compiler_params=pltpu.CompilerParams(vmem_limit_bytes=32 * 2**20),
        cost_estimate=pl.CostEstimate(
            flops=540_000_000, bytes_accessed=6_000_000, transcendentals=128
        ),
    )(att, weight, layer_input, gain)


def expert_kernel(quarters, place_ref, *refs):
    x_refs, w_refs = refs[:quarters], refs[quarters:-5 - quarters]
    out_refs = refs[-5 - quarters : -5]
    w_vmem, x_all, acc_ref, hid_ref, sems = refs[-5:]
    pieces = len(w_refs)
    depth = w_refs[0].shape[0]
    copies = [
        pltpu.make_async_copy(w_refs[j], w_vmem.at[j], sems.at[j]) for j in range(pieces)
    ]
    for copy in copies:
        copy.start()
    rows = x_refs[0].shape[0]
    for r in range(quarters):
        x_all[r * rows : (r + 1) * rows] = x_refs[r][...]
    both = acc_ref.shape[1]
    ffe = both // 2
    hid_ref[...] = jnp.zeros_like(hid_ref)
    for j in range(pieces):
        copies[j].wait()
        cols = pl.ds(pl.multiple_of(place_ref[j] * depth, depth), depth)
        part = jnp.dot(x_all[:, cols], w_vmem[j, :, :both], preferred_element_type=jnp.float32)
        if j == 0:
            acc_ref[...] = part
        else:
            acc_ref[...] += part
    gate = acc_ref[:, :ffe]
    up = acc_ref[:, ffe:]
    hid_ref[:, :ffe] = (gate / (1.0 + jnp.exp(-gate)) * up).astype(jnp.bfloat16)
    hid = hid_ref[...]
    for j in range(pieces):
        cols = pl.ds(pl.multiple_of(place_ref[j] * depth, depth), depth)
        made = lax.dot_general(
            hid, w_vmem[j, :, both:], (((1,), (1,)), ((), ())), preferred_element_type=jnp.float32
        ).astype(jnp.bfloat16)
        for r in range(quarters):
            out_refs[r][:, cols] = made[r * rows : (r + 1) * rows]


def expert(places, x, pieces, ffe):
    quarters = len(x)
    rows, width = x[0].shape
    depth, lanes = pieces[0].shape
    total = quarters * rows
    vmem = pl.BlockSpec(memory_space=pltpu.VMEM)
    return pl.pallas_call(
        functools.partial(expert_kernel, quarters),
        out_shape=[jax.ShapeDtypeStruct((rows, width), jnp.bfloat16)] * quarters,
        in_specs=[pl.BlockSpec(memory_space=pltpu.SMEM)]
        + [vmem] * quarters
        + [pl.BlockSpec(memory_space=pl.ANY)] * len(pieces),
        out_specs=[vmem] * quarters,
        scratch_shapes=[
            pltpu.VMEM((len(pieces), depth, lanes), jnp.bfloat16),
            pltpu.VMEM((total, width), jnp.bfloat16),
            pltpu.VMEM((total, 2 * ffe), jnp.float32),
            pltpu.VMEM((total, lanes - 2 * ffe), jnp.bfloat16),
            pltpu.SemaphoreType.DMA((len(pieces),)),
        ],
        compiler_params=pltpu.CompilerParams(vmem_limit_bytes=48 * 2**20),
        cost_estimate=pl.CostEstimate(
            flops=6 * total * width * ffe,
            bytes_accessed=6 * width * ffe + 4 * total * width,
            transcendentals=total * ffe,
        ),
    )(places, *x, *pieces)


def body(
    layer_input,
    queries,
    keys,
    values,
    out_weight,
    norm_gain,
    route_ids,
    route_weight,
    w_gate,
    w_up,
    w_down,
):
    tok = layer_input.shape[1]
    ctx = lax.axis_index("ctx")
    exp = lax.axis_index("exp")
    core, y, xh = ctx % 2, ctx // 2 % NY, ctx // (2 * NY)
    z, xl = exp // 2, exp % 2
    same_core = [[p * 2 + c for p in range(2 * NY)] for c in range(2)]

    ffe = w_gate.shape[2]
    lanes = -(-3 * ffe // HD) * HD
    down_rows = jnp.swapaxes(w_down, 1, 2)
    blank = jnp.zeros((w_gate.shape[1], lanes - 3 * ffe), w_gate.dtype)

    def local(e):
        return jnp.concatenate([w_gate[e], w_up[e], down_rows[e], blank], axis=1)

    first = core == 0
    zero, one = local(0), local(1)
    come = ctx_shift(jnp.where(first, one, zero), 0, 0, 1)
    piece = jnp.concatenate(
        [jnp.where(first, zero, come), jnp.where(first, come, one)], axis=0
    )
    far = ctx_shift(piece, 1, 0, 0)
    near_up, near_down = ctx_shift(piece, 0, 1, 0), ctx_shift(piece, 0, -1, 0)

    heads = jnp.stack([queries[0], keys[0], values[0]]).reshape(3, tok, -1, HD)
    heads = heads.transpose(2, 0, 1, 3)
    own = lax.all_to_all(heads, "ctx", 0, 0, axis_index_groups=same_core, tiled=True)
    other = ctx_shift(own[:, 1:], 0, 0, 1)
    attended = attend(core.reshape(1), own, other)
    attended, far, near_up, near_down = lax.optimization_barrier(
        (attended, far, near_up, near_down)
    )
    far_up, far_down = ctx_shift(far, 0, 1, 0), ctx_shift(far, 0, -1, 0)
    near_two = ctx_shift(near_up, 0, 1, 0)
    attended = lax.all_to_all(attended, "ctx", 0, 0, axis_index_groups=same_core, tiled=True)

    picks = jnp.concatenate([route_ids[0].T.astype(jnp.float32), route_weight[0].T], axis=0)
    picks = picks[None]
    for d in (1, 2, 4):
        picks = jnp.concatenate([picks, z_shift(picks, d)], axis=0)
    top = route_ids.shape[2]
    ids, weights = picks[:, :top], picks[:, top:]
    quarter = jnp.arange(4)
    wanted = (4 * z + ((2 * xl + core) ^ quarter)).astype(jnp.float32)
    hits = ids[:, None] == wanted[None, :, None, None]
    hit = jnp.sum(hits.astype(jnp.float32), axis=2)
    share = jnp.sum(jnp.where(hits, weights[:, None], 0.0), axis=2)
    before = (jnp.arange(tok)[:, None] < jnp.arange(tok)[None, :]).astype(jnp.bfloat16)
    rank = jnp.einsum(
        "drs,st->drt", hit.astype(jnp.bfloat16), before, preferred_element_type=jnp.float32
    )
    slots = jnp.arange(SLOT, dtype=jnp.float32)
    at_slot = rank[:, :, None, :] == slots[None, None, :, None]
    placing = jnp.where(at_slot, hit[:, :, None, :], 0.0).reshape(NZ, 4 * SLOT, tok)
    placing = placing.astype(jnp.bfloat16)
    merging = jnp.where(at_slot, share[:, :, None, :], 0.0).reshape(NZ, 4 * SLOT, tok)
    merging = merging.transpose(0, 2, 1).astype(jnp.bfloat16)

    residual, normed = project(attended, out_weight, layer_input[0], norm_gain[None])

    half = tok // 2
    blocks = {0: (normed[:half], normed[half:])}
    for d in (1, 2, 3):
        blocks[d] = tuple(z_shift(a, 1) for a in blocks[d - 1])
        blocks[NZ - d] = tuple(z_shift(a, -1) for a in blocks[(NZ - d + 1) % NZ])
        if d == 1:
            far_down, blocks[1] = lax.optimization_barrier((far_down, blocks[1]))
            far_two = ctx_shift(far_down, 0, -1, 0)
    blocks[4] = (z_shift(blocks[3][0], 1), z_shift(blocks[5][1], -1))
    spots = ((0, 0), (1, 0), (0, -1), (0, 1), (1, -1), (1, 1), (0, 2), (1, 2))
    pieces = [piece, far, near_up, near_down, far_up, far_down, near_two, far_two]
    places = jnp.stack([(xh + dx) % 2 * NY + (y + dy) % NY for dx, dy in spots])
    swaps = (lambda a: a, lambda a: ctx_shift(a, 0, 0, 1), x_swap, diag_swap)
    returned = {}
    for batch in BATCHES:
        rows = [
            jnp.dot(
                placing[d], jnp.concatenate(blocks[d], axis=0), preferred_element_type=jnp.float32
            ).astype(jnp.bfloat16)
            for d in batch
        ]
        arrived = []
        for r in range(4):
            quarter_rows = [a[r * SLOT : (r + 1) * SLOT] for a in rows]
            arrived.append(swaps[r](jnp.concatenate(quarter_rows, axis=0)))
        made = expert(places, arrived, pieces, ffe)
        back = [swaps[r](made[r]) for r in range(4)]
        for i, d in enumerate(batch):
            returned[d] = jnp.concatenate(
                [a[i * SLOT : (i + 1) * SLOT] for a in back], axis=0
            )

    def part(d, h):
        return jnp.dot(
            merging[d, h * half : (h + 1) * half], returned[d], preferred_element_type=jnp.float32
        )

    def narrow(a):
        return a.astype(jnp.bfloat16)

    def wide(a):
        return a.astype(jnp.float32)

    up = [z_shift(narrow(part(4, 0)), 1), None]
    down = [None, z_shift(narrow(part(4, 1)), -1)]
    for d in (3, 2, 1):
        for h in range(2):
            more = part(NZ - d, h)
            up[h] = z_shift(narrow(more if up[h] is None else more + wide(up[h])), 1)
            more = part(d, 1 - h)
            kept = down[1 - h]
            down[1 - h] = z_shift(narrow(more if kept is None else more + wide(kept)), -1)
    mixed = [
        narrow(wide(residual[h * half : (h + 1) * half]) + part(0, h) + wide(up[h]) + wide(down[h]))
        for h in range(2)
    ]
    return jnp.concatenate(mixed, axis=0)[None]


def solution(mesh):
    return jax.shard_map(
        body,
        mesh=mesh,
        in_specs=(
            P("exp", "ctx", None),
            P("exp", "ctx", None),
            P("exp", "ctx", None),
            P("exp", "ctx", None),
            P(),
            P(),
            P("exp", "ctx", None),
            P("exp", "ctx", None),
            P("exp", "ctx", None),
            P("exp", "ctx", None),
            P("exp", None, "ctx"),
        ),
        out_specs=P("exp", "ctx", None),
        check_vma=False,
    )
```

```python
import functools
import math

import jax
import jax.numpy as jnp
from jax import lax
from jax.experimental import pallas as pl
from jax.experimental.pallas import tpu as pltpu
from jax.sharding import PartitionSpec as P

HD = 128
SLOT = 32
NY = 4
NZ = 8
GROUPS = ((0, 1, 7), (2, 6), (3, 5), (4,))


def ctx_pairs(dx, dy, dc):
    pairs = []
    for i in range(16):
        xh, y, c = i // 8, i // 2 % NY, i % 2
        pairs.append((i, ((xh + dx) % 2 * NY + (y + dy) % NY) * 2 + (c + dc) % 2))
    return pairs


def z_pairs(d):
    return [(z * 2 + x, (z + d) % NZ * 2 + x) for z in range(NZ) for x in range(2)]


def ctx_shift(a, dx, dy, dc):
    return lax.ppermute(a, "ctx", ctx_pairs(dx, dy, dc))


def z_shift(a, d):
    return lax.ppermute(a, "exp", z_pairs(d))


def x_swap(a):
    return lax.ppermute(a, "exp", [(i, i ^ 1) for i in range(16)])


def diag_swap(a):
    pairs = [(c * 16 + e, (c ^ 1) * 16 + (e ^ 1)) for c in range(16) for e in range(16)]
    return lax.ppermute(a, ("ctx", "exp"), pairs)


def attend_kernel(core_ref, own_ref, other_ref, out_ref):
    count = own_ref.shape[0]
    core = core_ref[0]
    row = lax.broadcasted_iota(jnp.int32, (HD, HD), 0)
    col = lax.broadcasted_iota(jnp.int32, (HD, HD), 1)
    dims = (((1,), (1,)), ((), ()))
    scale = 1.0 / math.sqrt(HD)
    for p in range(count):
        q = own_ref[p, 0]
        width = (p + 1) * HD
        k_own = own_ref[: p + 1, 1].reshape(width, HD)
        v_own = own_ref[: p + 1, 2].reshape(width, HD)
        k_oth = other_ref[: p + 1, 1].reshape(width, HD)
        v_oth = other_ref[: p + 1, 2].reshape(width, HD)
        s_own = lax.dot_general(q, k_own, dims, preferred_element_type=jnp.float32) * scale
        s_oth = lax.dot_general(q, k_oth, dims, preferred_element_type=jnp.float32) * scale
        last_own = jnp.where(row >= col, s_own[:, p * HD :], -1e30)
        last_oth = jnp.where(core == 1, s_oth[:, p * HD :], -1e30)
        if p:
            s_own = jnp.concatenate([s_own[:, : p * HD], last_own], axis=1)
            s_oth = jnp.concatenate([s_oth[:, : p * HD], last_oth], axis=1)
        else:
            s_own, s_oth = last_own, last_oth
        top = jnp.maximum(
            jnp.max(s_own, axis=-1, keepdims=True), jnp.max(s_oth, axis=-1, keepdims=True)
        )
        e_own = jnp.exp(s_own - top)
        e_oth = jnp.exp(s_oth - top)
        total = jnp.sum(e_own, axis=-1, keepdims=True) + jnp.sum(e_oth, axis=-1, keepdims=True)
        acc = jnp.dot(e_own.astype(jnp.bfloat16), v_own, preferred_element_type=jnp.float32)
        acc += jnp.dot(e_oth.astype(jnp.bfloat16), v_oth, preferred_element_type=jnp.float32)
        out_ref[p] = (acc / total).astype(jnp.bfloat16)


def attend(core, own, other):
    count = own.shape[0]
    return pl.pallas_call(
        attend_kernel,
        out_shape=jax.ShapeDtypeStruct((count, HD, HD), jnp.bfloat16),
        in_specs=[
            pl.BlockSpec(memory_space=pltpu.SMEM),
            pl.BlockSpec(memory_space=pltpu.VMEM),
            pl.BlockSpec(memory_space=pltpu.VMEM),
        ],
        out_specs=pl.BlockSpec(memory_space=pltpu.VMEM),
        compiler_params=pltpu.CompilerParams(vmem_limit_bytes=16 * 2**20),
        cost_estimate=pl.CostEstimate(
            flops=700_000_000, bytes_accessed=1_600_000, transcendentals=1_200_000
        ),
    )(core, own, other)


def project_kernel(att_ref, weight_ref, input_ref, gain_ref, res_ref, normed_ref, w_vmem, sems):
    heads = att_ref.shape[0]
    width = weight_ref.shape[1]
    tile = w_vmem.shape[2]
    tiles = width // tile
    copies = [
        pltpu.make_async_copy(
            weight_ref.at[:, pl.ds(j * tile, tile)], w_vmem.at[j], sems.at[j]
        )
        for j in range(tiles)
    ]
    for copy in copies:
        copy.start()
    att = jnp.concatenate([att_ref[h] for h in range(heads)], axis=1)
    square = jnp.zeros((att.shape[0], 1), jnp.float32)
    for j in range(tiles):
        cols = slice(j * tile, (j + 1) * tile)
        copies[j].wait()
        part = jnp.dot(att, w_vmem[j], preferred_element_type=jnp.float32)
        part = (part + input_ref[:, cols].astype(jnp.float32)).astype(jnp.bfloat16)
        res_ref[:, cols] = part
        part = part.astype(jnp.float32)
        square += jnp.sum(part * part, axis=-1, keepdims=True)
    factor = lax.rsqrt(square / width + 1e-06)
    half = att.shape[0] // 2
    for j in range(tiles):
        cols = slice(j * tile, (j + 1) * tile)
        normed = (res_ref[:, cols].astype(jnp.float32) * factor * gain_ref[:, cols]).astype(
            jnp.bfloat16
        )
        for h in range(2):
            normed_ref[h, :, cols] = normed[h * half : (h + 1) * half]


def project(att, weight, layer_input, gain):
    rows, width = layer_input.shape
    vmem = pl.BlockSpec(memory_space=pltpu.VMEM)
    tile = 512
    return pl.pallas_call(
        project_kernel,
        out_shape=(
            jax.ShapeDtypeStruct((rows, width), jnp.bfloat16),
            jax.ShapeDtypeStruct((2, rows // 2, width), jnp.bfloat16),
        ),
        in_specs=[vmem, pl.BlockSpec(memory_space=pl.ANY), vmem, vmem],
        out_specs=(vmem, vmem),
        scratch_shapes=[
            pltpu.VMEM((width // tile, weight.shape[0], tile), jnp.bfloat16),
            pltpu.SemaphoreType.DMA((width // tile,)),
        ],
        compiler_params=pltpu.CompilerParams(vmem_limit_bytes=40 * 2**20),
        cost_estimate=pl.CostEstimate(
            flops=540_000_000, bytes_accessed=6_000_000, transcendentals=128
        ),
    )(att, weight, layer_input, gain)


def expert_kernel(spans, place_ref, *refs):
    count = len(spans)
    x_refs, w_refs, out_refs = refs[:count], refs[count : -5 - count], refs[-5 - count : -5]
    w_vmem, x_all, acc_ref, hid_ref, sems = refs[-5:]
    pieces = len(w_refs)
    depth = w_refs[0].shape[0]
    copies = [
        pltpu.make_async_copy(w_refs[j], w_vmem.at[j], sems.at[j]) for j in range(pieces)
    ]
    for copy in copies:
        copy.start()
    for x_ref, (at, size) in zip(x_refs, spans):
        x_all[at : at + size] = x_ref[...]
    both = acc_ref.shape[1]
    ffe = both // 2
    hid_ref[...] = jnp.zeros_like(hid_ref)
    for j in range(pieces):
        copies[j].wait()
        cols = pl.ds(pl.multiple_of(place_ref[j] * depth, depth), depth)
        part = jnp.dot(x_all[:, cols], w_vmem[j, :, :both], preferred_element_type=jnp.float32)
        if j == 0:
            acc_ref[...] = part
        else:
            acc_ref[...] += part
    gate = acc_ref[:, :ffe]
    up = acc_ref[:, ffe:]
    hid_ref[:, :ffe] = (gate / (1.0 + jnp.exp(-gate)) * up).astype(jnp.bfloat16)
    hid = hid_ref[...]
    for j in range(pieces):
        cols = pl.ds(pl.multiple_of(place_ref[j] * depth, depth), depth)
        made = lax.dot_general(
            hid, w_vmem[j, :, both:], (((1,), (1,)), ((), ())), preferred_element_type=jnp.float32
        ).astype(jnp.bfloat16)
        for out_ref, (at, size) in zip(out_refs, spans):
            out_ref[:, cols] = made[at : at + size]


def expert(places, x, pieces, ffe):
    width = x[0].shape[1]
    depth, lanes = pieces[0].shape
    spans, total = [], 0
    for a in x:
        spans.append((total, a.shape[0]))
        total += a.shape[0]
    vmem = pl.BlockSpec(memory_space=pltpu.VMEM)
    return pl.pallas_call(
        functools.partial(expert_kernel, tuple(spans)),
        out_shape=[jax.ShapeDtypeStruct(a.shape, jnp.bfloat16) for a in x],
        in_specs=[pl.BlockSpec(memory_space=pltpu.SMEM)]
        + [vmem] * len(x)
        + [pl.BlockSpec(memory_space=pl.ANY)] * len(pieces),
        out_specs=[vmem] * len(x),
        scratch_shapes=[
            pltpu.VMEM((len(pieces), depth, lanes), jnp.bfloat16),
            pltpu.VMEM((total, width), jnp.bfloat16),
            pltpu.VMEM((total, 2 * ffe), jnp.float32),
            pltpu.VMEM((total, lanes - 2 * ffe), jnp.bfloat16),
            pltpu.SemaphoreType.DMA((len(pieces),)),
        ],
        compiler_params=pltpu.CompilerParams(vmem_limit_bytes=40 * 2**20),
        cost_estimate=pl.CostEstimate(
            flops=6 * total * width * ffe,
            bytes_accessed=6 * width * ffe + 4 * total * width,
            transcendentals=total * ffe,
        ),
    )(places, *x, *pieces)


def body(
    layer_input,
    queries,
    keys,
    values,
    out_weight,
    norm_gain,
    route_ids,
    route_weight,
    w_gate,
    w_up,
    w_down,
):
    tok = layer_input.shape[1]
    ctx = lax.axis_index("ctx")
    exp = lax.axis_index("exp")
    core, y, xh = ctx % 2, ctx // 2 % NY, ctx // (2 * NY)
    z, xl = exp // 2, exp % 2
    same_core = [[p * 2 + c for p in range(2 * NY)] for c in range(2)]

    ffe = w_gate.shape[2]
    lanes = -(-3 * ffe // HD) * HD
    down_rows = jnp.swapaxes(w_down, 1, 2)
    blank = jnp.zeros((w_gate.shape[1], lanes - 3 * ffe), w_gate.dtype)

    def local(e):
        return jnp.concatenate([w_gate[e], w_up[e], down_rows[e], blank], axis=1)

    first = core == 0
    zero, one = local(0), local(1)
    come = ctx_shift(jnp.where(first, one, zero), 0, 0, 1)
    piece = jnp.concatenate(
        [jnp.where(first, zero, come), jnp.where(first, come, one)], axis=0
    )
    far = ctx_shift(piece, 1, 0, 0)
    near_up, near_down = ctx_shift(piece, 0, 1, 0), ctx_shift(piece, 0, -1, 0)

    picks = jnp.concatenate([route_ids[0].T.astype(jnp.float32), route_weight[0].T], axis=0)
    picks = picks[None]
    picks = jnp.concatenate([picks, z_shift(picks, 1)], axis=0)

    heads = jnp.stack([queries[0], keys[0], values[0]]).reshape(3, tok, -1, HD)
    heads = heads.transpose(2, 0, 1, 3)
    own = lax.all_to_all(heads, "ctx", 0, 0, axis_index_groups=same_core, tiled=True)
    own, picks = lax.optimization_barrier((own, picks))
    other = ctx_shift(own, 0, 0, 1)
    picks = jnp.concatenate([picks, z_shift(picks, 2)], axis=0)
    attended = attend(core.reshape(1), own, other)
    attended, picks = lax.optimization_barrier((attended, picks))
    picks = jnp.concatenate([picks, z_shift(picks, 4)], axis=0)
    attended = lax.all_to_all(attended, "ctx", 0, 0, axis_index_groups=same_core, tiled=True)
    attended, picks, far, near_up, near_down = lax.optimization_barrier(
        (attended, picks, far, near_up, near_down)
    )
    far_up, far_down = ctx_shift(far, 0, 1, 0), ctx_shift(far, 0, -1, 0)

    top = route_ids.shape[2]
    ids, weights = picks[:, :top], picks[:, top:]
    quarter = jnp.arange(4)
    wanted = (4 * z + ((2 * xl + core) ^ quarter)).astype(jnp.float32)
    hits = ids[:, None] == wanted[None, :, None, None]
    hit = jnp.sum(hits.astype(jnp.float32), axis=2)
    share = jnp.sum(jnp.where(hits, weights[:, None], 0.0), axis=2)
    before = (jnp.arange(tok)[:, None] < jnp.arange(tok)[None, :]).astype(jnp.bfloat16)
    rank = jnp.einsum(
        "drs,st->drt", hit.astype(jnp.bfloat16), before, preferred_element_type=jnp.float32
    )
    slots = jnp.arange(SLOT, dtype=jnp.float32)
    at_slot = rank[:, :, None, :] == slots[None, None, :, None]
    placing = jnp.where(at_slot, hit[:, :, None, :], 0.0).reshape(NZ, 4 * SLOT, tok)
    placing = placing.astype(jnp.bfloat16)
    merging = jnp.where(at_slot, share[:, :, None, :], 0.0).reshape(NZ, 4 * SLOT, tok)
    merging = merging.transpose(0, 2, 1).astype(jnp.bfloat16)

    residual, normed = project(attended, out_weight, layer_input[0], norm_gain[None])

    swaps = (lambda a: a, lambda a: ctx_shift(a, 0, 0, 1), x_swap, diag_swap)

    def rows_of(blocks):
        rows = [
            jnp.dot(
                placing[d], jnp.concatenate(blocks[d], axis=0), preferred_element_type=jnp.float32
            ).astype(jnp.bfloat16)
            for d in blocks
        ]
        return [
            swaps[r](jnp.concatenate([a[r * SLOT : (r + 1) * SLOT] for a in rows], axis=0))
            for r in range(4)
        ]

    half = tok // 2
    blocks = {0: (normed[0], normed[1])}
    rows = {}
    for d in (1, 2, 3):
        blocks[d] = tuple(z_shift(a, 1) for a in blocks[d - 1])
        blocks[NZ - d] = tuple(z_shift(a, -1) for a in blocks[(NZ - d + 1) % NZ])
        if d == 1:
            blocks, far_up, far_down = lax.optimization_barrier((blocks, far_up, far_down))
            near_two, far_two = ctx_shift(near_up, 0, 1, 0), ctx_shift(far_down, 0, -1, 0)
        elif d == 2:
            blocks, rows[0] = lax.optimization_barrier((blocks, rows[0]))
        else:
            blocks, rows[1], near_two, far_two = lax.optimization_barrier(
                (blocks, rows[1], near_two, far_two)
            )
        rows[d - 1] = rows_of({k: blocks[k] for k in GROUPS[d - 1]})
    blocks[4] = (z_shift(blocks[3][0], 1), z_shift(blocks[5][1], -1))
    spots = ((0, 0), (1, 0), (0, -1), (0, 1), (1, -1), (1, 1), (0, 2), (1, 2))
    pieces = [piece, far, near_up, near_down, far_up, far_down, near_two, far_two]
    places = jnp.stack([(xh + dx) % 2 * NY + (y + dy) % NY for dx, dy in spots])
    rows[3] = rows_of({4: blocks[4]})
    early = expert(places, rows[0] + rows[1], pieces, ffe)
    early, rows[2], rows[3] = lax.optimization_barrier((early, rows[2], rows[3]))
    made = {0: early[:4], 1: early[4:]}

    def send_back(g):
        made[g] = [swaps[r](made[g][r]) for r in range(4)]

    made[3] = expert(places, rows[3], pieces, ffe)
    send_back(3)
    made[2] = expert(places, rows[2], pieces, ffe)
    made[3], made[2] = lax.optimization_barrier((made[3], made[2]))
    for g in (2, 1, 0):
        send_back(g)

    def returned(d):
        g = next(i for i, group in enumerate(GROUPS) if d in group)
        i = GROUPS[g].index(d)
        return jnp.concatenate([a[i * SLOT : (i + 1) * SLOT] for a in made[g]], axis=0)

    def part(d, h):
        return jnp.dot(
            merging[d, h * half : (h + 1) * half], returned(d), preferred_element_type=jnp.float32
        )

    def narrow(a):
        return a.astype(jnp.bfloat16)

    def wide(a):
        return a.astype(jnp.float32)

    up = [z_shift(narrow(part(4, 0)), 1), None]
    down = [None, z_shift(narrow(part(4, 1)), -1)]
    up, down, made[2], made[1] = lax.optimization_barrier((up, down, made[2], made[1]))
    for d in (3, 2, 1):
        for h in range(2):
            more = part(NZ - d, h)
            up[h] = z_shift(narrow(more if up[h] is None else more + wide(up[h])), 1)
            more = part(d, 1 - h)
            kept = down[1 - h]
            down[1 - h] = z_shift(narrow(more if kept is None else more + wide(kept)), -1)
        if d == 3:
            up, down, made[0] = lax.optimization_barrier((up, down, made[0]))
    mixed = [
        narrow(wide(residual[h * half : (h + 1) * half]) + part(0, h) + wide(up[h]) + wide(down[h]))
        for h in range(2)
    ]
    return jnp.concatenate(mixed, axis=0)[None]


def solution(mesh):
    return jax.shard_map(
        body,
        mesh=mesh,
        in_specs=(
            P("exp", "ctx", None),
            P("exp", "ctx", None),
            P("exp", "ctx", None),
            P("exp", "ctx", None),
            P(),
            P(),
            P("exp", "ctx", None),
            P("exp", "ctx", None),
            P("exp", "ctx", None),
            P("exp", "ctx", None),
            P("exp", None, "ctx"),
        ),
        out_specs=P("exp", "ctx", None),
        check_vma=False,
    )
```

```python
import functools
import math

import jax
import jax.numpy as jnp
from jax import lax
from jax.experimental import pallas as pl
from jax.experimental.pallas import tpu as pltpu
from jax.sharding import PartitionSpec as P

HD = 128
SLOT = 32
NY = 4
NZ = 8
GROUPS = ((0, 1, 7), (2, 6), (3, 5), (4,))


def ctx_pairs(dx, dy, dc):
    pairs = []
    for i in range(16):
        xh, y, c = i // 8, i // 2 % NY, i % 2
        pairs.append((i, ((xh + dx) % 2 * NY + (y + dy) % NY) * 2 + (c + dc) % 2))
    return pairs


def z_pairs(d):
    return [(z * 2 + x, (z + d) % NZ * 2 + x) for z in range(NZ) for x in range(2)]


def ctx_shift(a, dx, dy, dc):
    return lax.ppermute(a, "ctx", ctx_pairs(dx, dy, dc))


def z_shift(a, d):
    return lax.ppermute(a, "exp", z_pairs(d))


def x_swap(a):
    return lax.ppermute(a, "exp", [(i, i ^ 1) for i in range(16)])


def diag_swap(a):
    pairs = [(c * 16 + e, (c ^ 1) * 16 + (e ^ 1)) for c in range(16) for e in range(16)]
    return lax.ppermute(a, ("ctx", "exp"), pairs)


def attend_kernel(core_ref, own_ref, other_ref, out_ref):
    count = own_ref.shape[0]
    core = core_ref[0]
    row = lax.broadcasted_iota(jnp.int32, (HD, HD), 0)
    col = lax.broadcasted_iota(jnp.int32, (HD, HD), 1)
    dims = (((1,), (1,)), ((), ()))
    scale = 1.0 / math.sqrt(HD)
    for p in range(count):
        q = own_ref[p, 0]
        width = (p + 1) * HD
        k_own = own_ref[: p + 1, 1].reshape(width, HD)
        v_own = own_ref[: p + 1, 2].reshape(width, HD)
        k_oth = other_ref[: p + 1, 1].reshape(width, HD)
        v_oth = other_ref[: p + 1, 2].reshape(width, HD)
        s_own = lax.dot_general(q, k_own, dims, preferred_element_type=jnp.float32) * scale
        s_oth = lax.dot_general(q, k_oth, dims, preferred_element_type=jnp.float32) * scale
        last_own = jnp.where(row >= col, s_own[:, p * HD :], -1e30)
        last_oth = jnp.where(core == 1, s_oth[:, p * HD :], -1e30)
        if p:
            s_own = jnp.concatenate([s_own[:, : p * HD], last_own], axis=1)
            s_oth = jnp.concatenate([s_oth[:, : p * HD], last_oth], axis=1)
        else:
            s_own, s_oth = last_own, last_oth
        top = jnp.maximum(
            jnp.max(s_own, axis=-1, keepdims=True), jnp.max(s_oth, axis=-1, keepdims=True)
        )
        e_own = jnp.exp(s_own - top)
        e_oth = jnp.exp(s_oth - top)
        total = jnp.sum(e_own, axis=-1, keepdims=True) + jnp.sum(e_oth, axis=-1, keepdims=True)
        acc = jnp.dot(e_own.astype(jnp.bfloat16), v_own, preferred_element_type=jnp.float32)
        acc += jnp.dot(e_oth.astype(jnp.bfloat16), v_oth, preferred_element_type=jnp.float32)
        out_ref[p] = (acc / total).astype(jnp.bfloat16)


def attend(core, own, other):
    count = own.shape[0]
    return pl.pallas_call(
        attend_kernel,
        out_shape=jax.ShapeDtypeStruct((count, HD, HD), jnp.bfloat16),
        in_specs=[
            pl.BlockSpec(memory_space=pltpu.SMEM),
            pl.BlockSpec(memory_space=pltpu.VMEM),
            pl.BlockSpec(memory_space=pltpu.VMEM),
        ],
        out_specs=pl.BlockSpec(memory_space=pltpu.VMEM),
        compiler_params=pltpu.CompilerParams(vmem_limit_bytes=16 * 2**20),
        cost_estimate=pl.CostEstimate(
            flops=700_000_000, bytes_accessed=1_600_000, transcendentals=1_200_000
        ),
    )(core, own, other)


def project_kernel(att_ref, weight_ref, input_ref, gain_ref, res_ref, top_ref, low_ref, w_vmem, sems):
    heads = att_ref.shape[0]
    width = weight_ref.shape[1]
    tile = w_vmem.shape[2]
    tiles = width // tile
    copies = [
        pltpu.make_async_copy(
            weight_ref.at[:, pl.ds(j * tile, tile)], w_vmem.at[j], sems.at[j]
        )
        for j in range(tiles)
    ]
    for copy in copies:
        copy.start()
    att = jnp.concatenate([att_ref[h] for h in range(heads)], axis=1)
    square = jnp.zeros((att.shape[0], 1), jnp.float32)
    for j in range(tiles):
        cols = slice(j * tile, (j + 1) * tile)
        copies[j].wait()
        part = jnp.dot(att, w_vmem[j], preferred_element_type=jnp.float32)
        part = (part + input_ref[:, cols].astype(jnp.float32)).astype(jnp.bfloat16)
        res_ref[:, cols] = part
        part = part.astype(jnp.float32)
        square += jnp.sum(part * part, axis=-1, keepdims=True)
    factor = lax.rsqrt(square / width + 1e-06)
    half = att.shape[0] // 2
    for j in range(tiles):
        cols = slice(j * tile, (j + 1) * tile)
        normed = (res_ref[:, cols].astype(jnp.float32) * factor * gain_ref[:, cols]).astype(
            jnp.bfloat16
        )
        top_ref[:, cols] = normed[:half]
        low_ref[:, cols] = normed[half:]


def project(att, weight, layer_input, gain):
    rows, width = layer_input.shape
    vmem = pl.BlockSpec(memory_space=pltpu.VMEM)
    tile = 512
    return pl.pallas_call(
        project_kernel,
        out_shape=(
            jax.ShapeDtypeStruct((rows, width), jnp.bfloat16),
            jax.ShapeDtypeStruct((rows // 2, width), jnp.bfloat16),
            jax.ShapeDtypeStruct((rows // 2, width), jnp.bfloat16),
        ),
        in_specs=[vmem, pl.BlockSpec(memory_space=pltpu.HBM), vmem, vmem],
        out_specs=(vmem, vmem, vmem),
        scratch_shapes=[
            pltpu.VMEM((width // tile, weight.shape[0], tile), jnp.bfloat16),
            pltpu.SemaphoreType.DMA((width // tile,)),
        ],
        compiler_params=pltpu.CompilerParams(vmem_limit_bytes=40 * 2**20),
        cost_estimate=pl.CostEstimate(
            flops=540_000_000, bytes_accessed=6_000_000, transcendentals=128
        ),
    )(att, weight, layer_input, gain)


def pick_kernel(group, placing_ref, *refs):
    block_refs, out_refs = refs[:-4], refs[-4:]
    width = out_refs[0].shape[1]
    tile = 512
    for i, d in enumerate(group):
        for j in range(width // tile):
            cols = slice(j * tile, (j + 1) * tile)
            block = jnp.concatenate(
                [block_refs[2 * i][:, cols], block_refs[2 * i + 1][:, cols]], axis=0
            )
            rows = jnp.dot(placing_ref[d], block, preferred_element_type=jnp.float32)
            rows = rows.astype(jnp.bfloat16)
            for r in range(4):
                out_refs[r][i * SLOT : (i + 1) * SLOT, cols] = rows[r * SLOT : (r + 1) * SLOT]


def pick(group, placing, halves):
    width = halves[0].shape[1]
    vmem = pl.BlockSpec(memory_space=pltpu.VMEM)
    rows = len(group) * SLOT
    return pl.pallas_call(
        functools.partial(pick_kernel, group),
        out_shape=[jax.ShapeDtypeStruct((rows, width), jnp.bfloat16)] * 4,
        in_specs=[vmem] * (1 + len(halves)),
        out_specs=[vmem] * 4,
        compiler_params=pltpu.CompilerParams(vmem_limit_bytes=16 * 2**20),
        cost_estimate=pl.CostEstimate(
            flops=2 * 4 * rows * HD * width, bytes_accessed=16 * rows * width, transcendentals=0
        ),
    )(placing, *halves)


def expert_kernel(spans, place_ref, *refs):
    count = len(spans)
    x_refs, w_refs, out_refs = refs[:count], refs[count : -5 - count], refs[-5 - count : -5]
    w_vmem, x_all, acc_ref, hid_ref, sems = refs[-5:]
    pieces = len(w_refs)
    depth = w_refs[0].shape[0]
    copies = [
        pltpu.make_async_copy(w_refs[j], w_vmem.at[j], sems.at[j]) for j in range(pieces)
    ]
    for copy in copies:
        copy.start()
    for x_ref, (at, size) in zip(x_refs, spans):
        x_all[at : at + size] = x_ref[...]
    both = acc_ref.shape[1]
    ffe = both // 2
    hid_ref[...] = jnp.zeros_like(hid_ref)
    for j in range(pieces):
        copies[j].wait()
        cols = pl.ds(pl.multiple_of(place_ref[j] * depth, depth), depth)
        part = jnp.dot(x_all[:, cols], w_vmem[j, :, :both], preferred_element_type=jnp.float32)
        if j == 0:
            acc_ref[...] = part
        else:
            acc_ref[...] += part
    gate = acc_ref[:, :ffe]
    up = acc_ref[:, ffe:]
    hid_ref[:, :ffe] = (gate / (1.0 + jnp.exp(-gate)) * up).astype(jnp.bfloat16)
    hid = hid_ref[...]
    for j in range(pieces):
        cols = pl.ds(pl.multiple_of(place_ref[j] * depth, depth), depth)
        made = lax.dot_general(
            hid, w_vmem[j, :, both:], (((1,), (1,)), ((), ())), preferred_element_type=jnp.float32
        ).astype(jnp.bfloat16)
        for out_ref, (at, size) in zip(out_refs, spans):
            out_ref[:, cols] = made[at : at + size]


def expert(places, x, pieces, ffe):
    width = x[0].shape[1]
    depth, lanes = pieces[0].shape
    spans, total = [], 0
    for a in x:
        spans.append((total, a.shape[0]))
        total += a.shape[0]
    vmem = pl.BlockSpec(memory_space=pltpu.VMEM)
    return pl.pallas_call(
        functools.partial(expert_kernel, tuple(spans)),
        out_shape=[jax.ShapeDtypeStruct(a.shape, jnp.bfloat16) for a in x],
        in_specs=[pl.BlockSpec(memory_space=pltpu.SMEM)]
        + [vmem] * len(x)
        + [pl.BlockSpec(memory_space=pltpu.HBM)] * len(pieces),
        out_specs=[vmem] * len(x),
        scratch_shapes=[
            pltpu.VMEM((len(pieces), depth, lanes), jnp.bfloat16),
            pltpu.VMEM((total, width), jnp.bfloat16),
            pltpu.VMEM((total, 2 * ffe), jnp.float32),
            pltpu.VMEM((total, lanes - 2 * ffe), jnp.bfloat16),
            pltpu.SemaphoreType.DMA((len(pieces),)),
        ],
        compiler_params=pltpu.CompilerParams(vmem_limit_bytes=40 * 2**20),
        cost_estimate=pl.CostEstimate(
            flops=6 * total * width * ffe,
            bytes_accessed=6 * width * ffe + 4 * total * width,
            transcendentals=total * ffe,
        ),
    )(places, *x, *pieces)


def body(
    layer_input,
    queries,
    keys,
    values,
    out_weight,
    norm_gain,
    route_ids,
    route_weight,
    w_gate,
    w_up,
    w_down,
):
    tok = layer_input.shape[1]
    ctx = lax.axis_index("ctx")
    exp = lax.axis_index("exp")
    core, y, xh = ctx % 2, ctx // 2 % NY, ctx // (2 * NY)
    z, xl = exp // 2, exp % 2
    same_core = [[p * 2 + c for p in range(2 * NY)] for c in range(2)]

    ffe = w_gate.shape[2]
    lanes = -(-3 * ffe // HD) * HD
    down_rows = jnp.swapaxes(w_down, 1, 2)
    blank = jnp.zeros((w_gate.shape[1], lanes - 3 * ffe), w_gate.dtype)

    def local(e):
        return jnp.concatenate([w_gate[e], w_up[e], down_rows[e], blank], axis=1)

    first = core == 0
    zero, one = local(0), local(1)
    come = ctx_shift(jnp.where(first, one, zero), 0, 0, 1)
    piece = jnp.concatenate(
        [jnp.where(first, zero, come), jnp.where(first, come, one)], axis=0
    )
    far = ctx_shift(piece, 1, 0, 0)
    near_up, near_down = ctx_shift(piece, 0, 1, 0), ctx_shift(piece, 0, -1, 0)

    picks = jnp.concatenate([route_ids[0].T.astype(jnp.float32), route_weight[0].T], axis=0)
    picks = picks[None]
    picks = jnp.concatenate([picks, z_shift(picks, 1)], axis=0)

    heads = jnp.stack([queries[0], keys[0], values[0]]).reshape(3, tok, -1, HD)
    heads = heads.transpose(2, 0, 1, 3)
    own = lax.all_to_all(heads, "ctx", 0, 0, axis_index_groups=same_core, tiled=True)
    own, picks = lax.optimization_barrier((own, picks))
    other = ctx_shift(own, 0, 0, 1)
    picks = jnp.concatenate([picks, z_shift(picks, 2)], axis=0)
    attended = attend(core.reshape(1), own, other)
    attended, picks = lax.optimization_barrier((attended, picks))
    picks = jnp.concatenate([picks, z_shift(picks, 4)], axis=0)
    attended = lax.all_to_all(attended, "ctx", 0, 0, axis_index_groups=same_core, tiled=True)
    attended, picks, far, near_up, near_down = lax.optimization_barrier(
        (attended, picks, far, near_up, near_down)
    )
    far_up, far_down = ctx_shift(far, 0, 1, 0), ctx_shift(far, 0, -1, 0)

    top = route_ids.shape[2]
    ids, weights = picks[:, :top], picks[:, top:]
    quarter = jnp.arange(4)
    wanted = (4 * z + ((2 * xl + core) ^ quarter)).astype(jnp.float32)
    hits = ids[:, None] == wanted[None, :, None, None]
    hit = jnp.sum(hits.astype(jnp.float32), axis=2)
    share = jnp.sum(jnp.where(hits, weights[:, None], 0.0), axis=2)
    before = (jnp.arange(tok)[:, None] < jnp.arange(tok)[None, :]).astype(jnp.bfloat16)
    rank = jnp.einsum(
        "drs,st->drt", hit.astype(jnp.bfloat16), before, preferred_element_type=jnp.float32
    )
    slots = jnp.arange(SLOT, dtype=jnp.float32)
    at_slot = rank[:, :, None, :] == slots[None, None, :, None]
    placing = jnp.where(at_slot, hit[:, :, None, :], 0.0).reshape(NZ, 4 * SLOT, tok)
    placing = placing.astype(jnp.bfloat16)
    merging = jnp.where(at_slot, share[:, :, None, :], 0.0).reshape(NZ, 4 * SLOT, tok)
    merging = merging.transpose(0, 2, 1).astype(jnp.bfloat16)

    residual, top_half, low_half = project(attended, out_weight, layer_input[0], norm_gain[None])

    swaps = (lambda a: a, lambda a: ctx_shift(a, 0, 0, 1), x_swap, diag_swap)

    def swap_all(quarters):
        return [swaps[r](quarters[r]) for r in range(4)]

    def picked(g, halves):
        return pick(GROUPS[g], placing, halves)

    half = tok // 2
    blocks = {0: (top_half, low_half)}
    for d in (1, 2, 3):
        blocks[d] = tuple(z_shift(a, 1) for a in blocks[d - 1])
        blocks[NZ - d] = tuple(z_shift(a, -1) for a in blocks[(NZ - d + 1) % NZ])
    blocks[4] = (z_shift(blocks[3][0], 1), z_shift(blocks[5][1], -1))
    halves = [[a for d in group for a in blocks[d]] for group in GROUPS]
    rows = {0: swap_all(picked(0, halves[0]))}
    halves[1], rows[0], far_up, far_down = lax.optimization_barrier(
        (halves[1], rows[0], far_up, far_down)
    )
    near_two, far_two = ctx_shift(near_up, 0, 1, 0), ctx_shift(far_down, 0, -1, 0)
    rows[1] = swap_all(picked(1, halves[1]))
    halves[2], rows[1], near_two, far_two = lax.optimization_barrier(
        (halves[2], rows[1], near_two, far_two)
    )
    rows[2] = swap_all(picked(2, halves[2]))
    spots = ((0, 0), (1, 0), (0, -1), (0, 1), (1, -1), (1, 1), (0, 2), (1, 2))
    pieces = [piece, far, near_up, near_down, far_up, far_down, near_two, far_two]
    places = jnp.stack([(xh + dx) % 2 * NY + (y + dy) % NY for dx, dy in spots])
    last = picked(3, halves[3])
    rows[0], last = lax.optimization_barrier((rows[0], last))
    rows[3] = swap_all(last)
    early = expert(places, rows[0] + rows[1], pieces, ffe)
    early, rows[2], rows[3] = lax.optimization_barrier((early, rows[2], rows[3]))
    made = {0: early[:4], 1: early[4:]}

    def send_back(g):
        made[g] = [swaps[r](made[g][r]) for r in range(4)]

    made[3] = expert(places, rows[3], pieces, ffe)
    send_back(3)
    made[2] = expert(places, rows[2], pieces, ffe)
    made[3], made[2] = lax.optimization_barrier((made[3], made[2]))
    for g in (2, 1, 0):
        send_back(g)

    def returned(d):
        g = next(i for i, group in enumerate(GROUPS) if d in group)
        i = GROUPS[g].index(d)
        return jnp.concatenate([a[i * SLOT : (i + 1) * SLOT] for a in made[g]], axis=0)

    def part(d, h):
        return jnp.dot(
            merging[d, h * half : (h + 1) * half], returned(d), preferred_element_type=jnp.float32
        )

    def narrow(a):
        return a.astype(jnp.bfloat16)

    def wide(a):
        return a.astype(jnp.float32)

    up = [z_shift(narrow(part(4, 0)), 1), None]
    down = [None, z_shift(narrow(part(4, 1)), -1)]
    for d in (3, 2, 1):
        for h in range(2):
            more = part(NZ - d, h)
            up[h] = z_shift(narrow(more if up[h] is None else more + wide(up[h])), 1)
            more = part(d, 1 - h)
            kept = down[1 - h]
            down[1 - h] = z_shift(narrow(more if kept is None else more + wide(kept)), -1)
        if d == 3:
            up, down, made[0] = lax.optimization_barrier((up, down, made[0]))
    mixed = [
        narrow(wide(residual[h * half : (h + 1) * half]) + part(0, h) + wide(up[h]) + wide(down[h]))
        for h in range(2)
    ]
    return jnp.concatenate(mixed, axis=0)[None]


def solution(mesh):
    return jax.shard_map(
        body,
        mesh=mesh,
        in_specs=(
            P("exp", "ctx", None),
            P("exp", "ctx", None),
            P("exp", "ctx", None),
            P("exp", "ctx", None),
            P(),
            P(),
            P("exp", "ctx", None),
            P("exp", "ctx", None),
            P("exp", "ctx", None),
            P("exp", "ctx", None),
            P("exp", None, "ctx"),
        ),
        out_specs=P("exp", "ctx", None),
        check_vma=False,
    )
```

```python
import functools
import math

import jax
import jax.numpy as jnp
from jax import lax
from jax.experimental import pallas as pl
from jax.experimental.pallas import tpu as pltpu
from jax.sharding import PartitionSpec as P

HD = 128
SLOT = 32
NY = 4
NZ = 8
GROUPS = ((0, 1, 7), (2, 6), (3, 5), (4,))


def ctx_pairs(dx, dy, dc):
    pairs = []
    for i in range(16):
        xh, y, c = i // 8, i // 2 % NY, i % 2
        pairs.append((i, ((xh + dx) % 2 * NY + (y + dy) % NY) * 2 + (c + dc) % 2))
    return pairs


def z_pairs(d):
    return [(z * 2 + x, (z + d) % NZ * 2 + x) for z in range(NZ) for x in range(2)]


def ctx_shift(a, dx, dy, dc):
    return lax.ppermute(a, "ctx", ctx_pairs(dx, dy, dc))


def z_shift(a, d):
    return lax.ppermute(a, "exp", z_pairs(d))


def x_swap(a):
    return lax.ppermute(a, "exp", [(i, i ^ 1) for i in range(16)])


def diag_swap(a):
    pairs = [(c * 16 + e, (c ^ 1) * 16 + (e ^ 1)) for c in range(16) for e in range(16)]
    return lax.ppermute(a, ("ctx", "exp"), pairs)


def attend_kernel(core_ref, own_ref, other_ref, out_ref):
    count = own_ref.shape[0]
    core = core_ref[0]
    row = lax.broadcasted_iota(jnp.int32, (HD, HD), 0)
    col = lax.broadcasted_iota(jnp.int32, (HD, HD), 1)
    dims = (((1,), (1,)), ((), ()))
    scale = 1.0 / math.sqrt(HD)
    for p in range(count):
        q = own_ref[p, 0]
        width = (p + 1) * HD
        k_own = own_ref[: p + 1, 1].reshape(width, HD)
        v_own = own_ref[: p + 1, 2].reshape(width, HD)
        k_oth = other_ref[: p + 1, 1].reshape(width, HD)
        v_oth = other_ref[: p + 1, 2].reshape(width, HD)
        s_own = lax.dot_general(q, k_own, dims, preferred_element_type=jnp.float32) * scale
        s_oth = lax.dot_general(q, k_oth, dims, preferred_element_type=jnp.float32) * scale
        last_own = jnp.where(row >= col, s_own[:, p * HD :], -1e30)
        last_oth = jnp.where(core == 1, s_oth[:, p * HD :], -1e30)
        if p:
            s_own = jnp.concatenate([s_own[:, : p * HD], last_own], axis=1)
            s_oth = jnp.concatenate([s_oth[:, : p * HD], last_oth], axis=1)
        else:
            s_own, s_oth = last_own, last_oth
        top = jnp.maximum(
            jnp.max(s_own, axis=-1, keepdims=True), jnp.max(s_oth, axis=-1, keepdims=True)
        )
        e_own = jnp.exp(s_own - top)
        e_oth = jnp.exp(s_oth - top)
        total = jnp.sum(e_own, axis=-1, keepdims=True) + jnp.sum(e_oth, axis=-1, keepdims=True)
        acc = jnp.dot(e_own.astype(jnp.bfloat16), v_own, preferred_element_type=jnp.float32)
        acc += jnp.dot(e_oth.astype(jnp.bfloat16), v_oth, preferred_element_type=jnp.float32)
        out_ref[p] = (acc / total).astype(jnp.bfloat16)


def attend(core, own, other):
    count = own.shape[0]
    return pl.pallas_call(
        attend_kernel,
        out_shape=jax.ShapeDtypeStruct((count, HD, HD), jnp.bfloat16),
        in_specs=[
            pl.BlockSpec(memory_space=pltpu.SMEM),
            pl.BlockSpec(memory_space=pltpu.VMEM),
            pl.BlockSpec(memory_space=pltpu.VMEM),
        ],
        out_specs=pl.BlockSpec(memory_space=pltpu.VMEM),
        compiler_params=pltpu.CompilerParams(vmem_limit_bytes=16 * 2**20),
        cost_estimate=pl.CostEstimate(
            flops=700_000_000, bytes_accessed=1_600_000, transcendentals=1_200_000
        ),
    )(core, own, other)


def project_kernel(att_ref, weight_ref, input_ref, gain_ref, res_ref, normed_ref, w_vmem, sems):
    heads = att_ref.shape[0]
    width = weight_ref.shape[1]
    tile = w_vmem.shape[2]
    tiles = width // tile
    copies = [
        pltpu.make_async_copy(
            weight_ref.at[:, pl.ds(j * tile, tile)], w_vmem.at[j], sems.at[j]
        )
        for j in range(tiles)
    ]
    for copy in copies:
        copy.start()
    att = jnp.concatenate([att_ref[h] for h in range(heads)], axis=1)
    square = jnp.zeros((att.shape[0], 1), jnp.float32)
    for j in range(tiles):
        cols = slice(j * tile, (j + 1) * tile)
        copies[j].wait()
        part = jnp.dot(att, w_vmem[j], preferred_element_type=jnp.float32)
        part = (part + input_ref[:, cols].astype(jnp.float32)).astype(jnp.bfloat16)
        res_ref[:, cols] = part
        part = part.astype(jnp.float32)
        square += jnp.sum(part * part, axis=-1, keepdims=True)
    factor = lax.rsqrt(square / width + 1e-06)
    for j in range(tiles):
        cols = slice(j * tile, (j + 1) * tile)
        normed_ref[:, cols] = (
            res_ref[:, cols].astype(jnp.float32) * factor * gain_ref[:, cols]
        ).astype(jnp.bfloat16)


def project(att, weight, layer_input, gain):
    rows, width = layer_input.shape
    vmem = pl.BlockSpec(memory_space=pltpu.VMEM)
    tile = 512
    return pl.pallas_call(
        project_kernel,
        out_shape=(jax.ShapeDtypeStruct((rows, width), jnp.bfloat16),) * 2,
        in_specs=[vmem, pl.BlockSpec(memory_space=pltpu.HBM), vmem, vmem],
        out_specs=(vmem, vmem),
        scratch_shapes=[
            pltpu.VMEM((width // tile, weight.shape[0], tile), jnp.bfloat16),
            pltpu.SemaphoreType.DMA((width // tile,)),
        ],
        compiler_params=pltpu.CompilerParams(vmem_limit_bytes=60 * 2**20),
        cost_estimate=pl.CostEstimate(
            flops=540_000_000, bytes_accessed=6_000_000, transcendentals=128
        ),
    )(att, weight, layer_input, gain)


def pick_kernel(group, placing_ref, *refs):
    count = len(group)
    block_refs, (own_ref, core_ref, side_ref, held, sems) = refs[:count], refs[count:]
    width = own_ref.shape[1]
    size = count * SLOT
    copies = [
        pltpu.make_async_copy(block_refs[i], held.at[i], sems.at[i]) for i in range(count)
    ]
    for copy in copies:
        copy.start()
    tile = 512
    for i, d in enumerate(group):
        copies[i].wait()
        for j in range(width // tile):
            cols = slice(j * tile, (j + 1) * tile)
            rows = jnp.dot(placing_ref[d], held[i, :, cols], preferred_element_type=jnp.float32)
            rows = rows.astype(jnp.bfloat16)
            at = i * SLOT
            own_ref[at : at + SLOT, cols] = rows[:SLOT]
            core_ref[at : at + SLOT, cols] = rows[SLOT : 2 * SLOT]
            side_ref[at : at + SLOT, cols] = rows[2 * SLOT : 3 * SLOT]
            side_ref[size + at : size + at + SLOT, cols] = rows[3 * SLOT :]


def pick(group, placing, blocks):
    tok, width = blocks[0].shape
    vmem = pl.BlockSpec(memory_space=pltpu.VMEM)
    rows = len(group) * SLOT
    return pl.pallas_call(
        functools.partial(pick_kernel, group),
        out_shape=[jax.ShapeDtypeStruct((k * rows, width), jnp.bfloat16) for k in (1, 1, 2)],
        in_specs=[vmem] + [pl.BlockSpec(memory_space=pltpu.HBM)] * len(blocks),
        out_specs=[vmem] * 3,
        scratch_shapes=[
            pltpu.VMEM((len(blocks), tok, width), jnp.bfloat16),
            pltpu.SemaphoreType.DMA((len(blocks),)),
        ],
        compiler_params=pltpu.CompilerParams(vmem_limit_bytes=60 * 2**20),
        cost_estimate=pl.CostEstimate(
            flops=2 * 4 * rows * HD * width, bytes_accessed=16 * rows * width, transcendentals=0
        ),
    )(placing, *blocks)


def expert_kernel(spans, place_ref, *refs):
    count = len(spans)
    x_refs, w_refs, out_refs = refs[:count], refs[count : -5 - count], refs[-5 - count : -5]
    w_vmem, x_all, acc_ref, hid_ref, sems = refs[-5:]
    pieces = len(w_refs)
    depth = w_refs[0].shape[0]
    copies = [
        pltpu.make_async_copy(w_refs[j], w_vmem.at[j], sems.at[j]) for j in range(pieces)
    ]
    for copy in copies:
        copy.start()
    for x_ref, (at, size) in zip(x_refs, spans):
        x_all[at : at + size] = x_ref[...]
    both = acc_ref.shape[1]
    ffe = both // 2
    hid_ref[...] = jnp.zeros_like(hid_ref)
    for j in range(pieces):
        copies[j].wait()
        cols = pl.ds(pl.multiple_of(place_ref[j] * depth, depth), depth)
        part = jnp.dot(x_all[:, cols], w_vmem[j, :, :both], preferred_element_type=jnp.float32)
        if j == 0:
            acc_ref[...] = part
        else:
            acc_ref[...] += part
    gate = acc_ref[:, :ffe]
    up = acc_ref[:, ffe:]
    hid_ref[:, :ffe] = (gate / (1.0 + jnp.exp(-gate)) * up).astype(jnp.bfloat16)
    hid = hid_ref[...]
    for j in range(pieces):
        cols = pl.ds(pl.multiple_of(place_ref[j] * depth, depth), depth)
        made = lax.dot_general(
            hid, w_vmem[j, :, both:], (((1,), (1,)), ((), ())), preferred_element_type=jnp.float32
        ).astype(jnp.bfloat16)
        for out_ref, (at, size) in zip(out_refs, spans):
            out_ref[:, cols] = made[at : at + size]


def expert(places, x, pieces, ffe):
    width = x[0].shape[1]
    depth, lanes = pieces[0].shape
    spans, total = [], 0
    for a in x:
        spans.append((total, a.shape[0]))
        total += a.shape[0]
    vmem = pl.BlockSpec(memory_space=pltpu.VMEM)
    return pl.pallas_call(
        functools.partial(expert_kernel, tuple(spans)),
        out_shape=[jax.ShapeDtypeStruct(a.shape, jnp.bfloat16) for a in x],
        in_specs=[pl.BlockSpec(memory_space=pltpu.SMEM)]
        + [vmem] * len(x)
        + [pl.BlockSpec(memory_space=pltpu.HBM)] * len(pieces),
        out_specs=[vmem] * len(x),
        scratch_shapes=[
            pltpu.VMEM((len(pieces), depth, lanes), jnp.bfloat16),
            pltpu.VMEM((total, width), jnp.bfloat16),
            pltpu.VMEM((total, 2 * ffe), jnp.float32),
            pltpu.VMEM((total, lanes - 2 * ffe), jnp.bfloat16),
            pltpu.SemaphoreType.DMA((len(pieces),)),
        ],
        compiler_params=pltpu.CompilerParams(vmem_limit_bytes=60 * 2**20),
        cost_estimate=pl.CostEstimate(
            flops=6 * total * width * ffe,
            bytes_accessed=6 * width * ffe + 4 * total * width,
            transcendentals=total * ffe,
        ),
    )(places, *x, *pieces)


def body(
    layer_input,
    queries,
    keys,
    values,
    out_weight,
    norm_gain,
    route_ids,
    route_weight,
    w_gate,
    w_up,
    w_down,
):
    tok = layer_input.shape[1]
    ctx = lax.axis_index("ctx")
    exp = lax.axis_index("exp")
    core, y, xh = ctx % 2, ctx // 2 % NY, ctx // (2 * NY)
    z, xl = exp // 2, exp % 2
    same_core = [[p * 2 + c for p in range(2 * NY)] for c in range(2)]

    ffe = w_gate.shape[2]
    lanes = -(-3 * ffe // HD) * HD
    down_rows = jnp.swapaxes(w_down, 1, 2)
    blank = jnp.zeros((w_gate.shape[1], lanes - 3 * ffe), w_gate.dtype)

    def local(e):
        return jnp.concatenate([w_gate[e], w_up[e], down_rows[e], blank], axis=1)

    first = core == 0
    zero, one = local(0), local(1)
    come = ctx_shift(jnp.where(first, one, zero), 0, 0, 1)
    piece = jnp.concatenate(
        [jnp.where(first, zero, come), jnp.where(first, come, one)], axis=0
    )
    far = ctx_shift(piece, 1, 0, 0)
    near_up, near_down = ctx_shift(piece, 0, 1, 0), ctx_shift(piece, 0, -1, 0)

    picks = jnp.concatenate([route_ids[0].T.astype(jnp.float32), route_weight[0].T], axis=0)
    picks = picks[None]
    picks = jnp.concatenate([picks, z_shift(picks, 1)], axis=0)

    heads = jnp.stack([queries[0], keys[0], values[0]]).reshape(3, tok, -1, HD)
    heads = heads.transpose(2, 0, 1, 3)
    own = lax.all_to_all(heads, "ctx", 0, 0, axis_index_groups=same_core, tiled=True)
    own, picks = lax.optimization_barrier((own, picks))
    other = ctx_shift(own, 0, 0, 1)
    picks = jnp.concatenate([picks, z_shift(picks, 2)], axis=0)
    attended = attend(core.reshape(1), own, other)
    attended, picks = lax.optimization_barrier((attended, picks))
    picks = jnp.concatenate([picks, z_shift(picks, 4)], axis=0)
    attended = lax.all_to_all(attended, "ctx", 0, 0, axis_index_groups=same_core, tiled=True)
    attended, picks, far, near_up, near_down = lax.optimization_barrier(
        (attended, picks, far, near_up, near_down)
    )
    far_up, far_down = ctx_shift(far, 0, 1, 0), ctx_shift(far, 0, -1, 0)

    top = route_ids.shape[2]
    ids, weights = picks[:, :top], picks[:, top:]
    quarter = jnp.arange(4)
    wanted = (4 * z + ((2 * xl + core) ^ quarter)).astype(jnp.float32)
    hits = ids[:, None] == wanted[None, :, None, None]
    hit = jnp.sum(hits.astype(jnp.float32), axis=2)
    share = jnp.sum(jnp.where(hits, weights[:, None], 0.0), axis=2)
    before = (jnp.arange(tok)[:, None] < jnp.arange(tok)[None, :]).astype(jnp.bfloat16)
    rank = jnp.einsum(
        "drs,st->drt", hit.astype(jnp.bfloat16), before, preferred_element_type=jnp.float32
    )
    slots = jnp.arange(SLOT, dtype=jnp.float32)
    at_slot = rank[:, :, None, :] == slots[None, None, :, None]
    placing = jnp.where(at_slot, hit[:, :, None, :], 0.0).reshape(NZ, 4 * SLOT, tok)
    placing = placing.astype(jnp.bfloat16)
    merging = jnp.where(at_slot, share[:, :, None, :], 0.0).reshape(NZ, 4 * SLOT, tok)
    merging = merging.transpose(0, 2, 1).astype(jnp.bfloat16)

    residual, normed = project(attended, out_weight, layer_input[0], norm_gain[None])

    swaps = (lambda a: a, lambda a: ctx_shift(a, 0, 0, 1), x_swap, diag_swap)

    half = tok // 2
    blocks = {0: normed}
    for d in (1, 2, 3):
        blocks[d] = z_shift(blocks[d - 1], 1)
        blocks[NZ - d] = z_shift(blocks[(NZ - d + 1) % NZ], -1)
    blocks[4] = jnp.concatenate(
        [z_shift(blocks[3][:half], 1), z_shift(blocks[5][half:], -1)], axis=0
    )
    inputs = [[blocks[d] for d in group] for group in GROUPS]
    sizes = [len(group) * SLOT for group in GROUPS]
    own, cross, side = {}, {}, {}

    def send(g):
        own[g], cross[g], leaving = pick(GROUPS[g], placing, inputs[g])
        side[g] = x_swap(leaving)

    def over_cores(groups, a, b):
        both = swaps[1](jnp.concatenate([a[g] for g in groups] + [b[g] for g in groups], axis=0))
        out, at = [], 0
        for _ in range(2):
            parts = {}
            for g in groups:
                parts[g] = both[at : at + sizes[g]]
                at += sizes[g]
            out.append(parts)
        return out

    send(0)
    inputs[1], side[0], far_up, far_down = lax.optimization_barrier(
        (inputs[1], side[0], far_up, far_down)
    )
    near_two, far_two = ctx_shift(near_up, 0, 1, 0), ctx_shift(far_down, 0, -1, 0)
    send(1)
    inputs[2], side[1] = lax.optimization_barrier((inputs[2], side[1]))
    send(2)
    inputs[3], near_two, far_two = lax.optimization_barrier((inputs[3], near_two, far_two))
    spots = ((0, 0), (1, 0), (0, -1), (0, 1), (1, -1), (1, 1), (0, 2), (1, 2))
    pieces = [piece, far, near_up, near_down, far_up, far_down, near_two, far_two]
    places = jnp.stack([(xh + dx) % 2 * NY + (y + dy) % NY for dx, dy in spots])

    def halves_of(g):
        return side[g][: sizes[g]], side[g][sizes[g] :]

    straight, slant = {}, {}
    for g in (0, 1):
        straight[g], slant[g] = halves_of(g)
    core_rows, far_rows = over_cores((0, 1), cross, slant)
    last = pick(GROUPS[3], placing, inputs[3])
    core_rows, last = lax.optimization_barrier((core_rows, last))
    final = [
        last[0],
        swaps[1](last[1]),
        x_swap(last[2][: sizes[3]]),
        diag_swap(last[2][sizes[3] :]),
    ]
    early = expert(
        places,
        [kind[g] for kind in (own, straight, core_rows, far_rows) for g in (0, 1)],
        pieces,
        ffe,
    )
    early, side[2], final = lax.optimization_barrier((early, side[2], final))
    final = expert(places, final, pieces, ffe)
    final = [swaps[r](final[r]) for r in range(4)]
    straight[2], slant[2] = halves_of(2)
    core_rows, far_rows = over_cores((2,), cross, slant)
    middle = expert(
        places, [own[2], straight[2], core_rows[2], far_rows[2]], pieces, ffe
    )
    final, middle = lax.optimization_barrier((final, middle))
    done = {3: final}
    own[2], straight[2] = middle[:2]
    own[0], own[1], straight[0], straight[1] = early[:4]

    def send_back(groups, core_rows, far_rows):
        core_back, far_back = over_cores(groups, core_rows, far_rows)
        for g in groups:
            side_back = x_swap(jnp.concatenate([straight[g], far_back[g]], axis=0))
            done[g] = [own[g], core_back[g], side_back[: sizes[g]], side_back[sizes[g] :]]

    send_back((2,), {2: middle[2]}, {2: middle[3]})
    send_back((0, 1), {0: early[4], 1: early[5]}, {0: early[6], 1: early[7]})

    def returned(d):
        g = next(i for i, group in enumerate(GROUPS) if d in group)
        i = GROUPS[g].index(d)
        return jnp.concatenate([a[i * SLOT : (i + 1) * SLOT] for a in done[g]], axis=0)

    def part(d, h):
        return jnp.dot(
            merging[d, h * half : (h + 1) * half], returned(d), preferred_element_type=jnp.float32
        )

    def narrow(a):
        return a.astype(jnp.bfloat16)

    def wide(a):
        return a.astype(jnp.float32)

    up = [z_shift(narrow(part(4, 0)), 1), None]
    down = [None, z_shift(narrow(part(4, 1)), -1)]
    up, down, done[2], done[1] = lax.optimization_barrier((up, down, done[2], done[1]))
    for d in (3, 2, 1):
        for h in range(2):
            more = part(NZ - d, h)
            up[h] = z_shift(narrow(more if up[h] is None else more + wide(up[h])), 1)
            more = part(d, 1 - h)
            kept = down[1 - h]
            down[1 - h] = z_shift(narrow(more if kept is None else more + wide(kept)), -1)
        if d == 3:
            up, down, done[0] = lax.optimization_barrier((up, down, done[0]))
    mixed = [
        narrow(wide(residual[h * half : (h + 1) * half]) + part(0, h) + wide(up[h]) + wide(down[h]))
        for h in range(2)
    ]
    return jnp.concatenate(mixed, axis=0)[None]


def solution(mesh):
    return jax.shard_map(
        body,
        mesh=mesh,
        in_specs=(
            P("exp", "ctx", None),
            P("exp", "ctx", None),
            P("exp", "ctx", None),
            P("exp", "ctx", None),
            P(),
            P(),
            P("exp", "ctx", None),
            P("exp", "ctx", None),
            P("exp", "ctx", None),
            P("exp", "ctx", None),
            P("exp", None, "ctx"),
        ),
        out_specs=P("exp", "ctx", None),
        check_vma=False,
    )
```

```python
import functools
import math

import jax
import jax.numpy as jnp
from jax import lax
from jax.experimental import pallas as pl
from jax.experimental.pallas import tpu as pltpu
from jax.sharding import PartitionSpec as P

HD = 128
SLOT = 32
NY = 4
NZ = 8
GROUPS = ((0, 1, 7), (2, 6), (3, 5), (4,))


def ctx_pairs(dx, dy, dc):
    pairs = []
    for i in range(16):
        xh, y, c = i // 8, i // 2 % NY, i % 2
        pairs.append((i, ((xh + dx) % 2 * NY + (y + dy) % NY) * 2 + (c + dc) % 2))
    return pairs


def z_pairs(d):
    return [(z * 2 + x, (z + d) % NZ * 2 + x) for z in range(NZ) for x in range(2)]


def ctx_shift(a, dx, dy, dc):
    return lax.ppermute(a, "ctx", ctx_pairs(dx, dy, dc))


def z_shift(a, d):
    return lax.ppermute(a, "exp", z_pairs(d))


def x_swap(a):
    return lax.ppermute(a, "exp", [(i, i ^ 1) for i in range(16)])


def diag_swap(a):
    pairs = [(c * 16 + e, (c ^ 1) * 16 + (e ^ 1)) for c in range(16) for e in range(16)]
    return lax.ppermute(a, ("ctx", "exp"), pairs)


def attend_kernel(core_ref, own_ref, other_ref, out_ref):
    count = own_ref.shape[0]
    core = core_ref[0]
    row = lax.broadcasted_iota(jnp.int32, (HD, HD), 0)
    col = lax.broadcasted_iota(jnp.int32, (HD, HD), 1)
    dims = (((1,), (1,)), ((), ()))
    scale = 1.0 / math.sqrt(HD)
    for p in range(count):
        q = own_ref[p, 0]
        width = (p + 1) * HD
        k_own = own_ref[: p + 1, 1].reshape(width, HD)
        v_own = own_ref[: p + 1, 2].reshape(width, HD)
        k_oth = other_ref[: p + 1, 1].reshape(width, HD)
        v_oth = other_ref[: p + 1, 2].reshape(width, HD)
        s_own = lax.dot_general(q, k_own, dims, preferred_element_type=jnp.float32) * scale
        s_oth = lax.dot_general(q, k_oth, dims, preferred_element_type=jnp.float32) * scale
        last_own = jnp.where(row >= col, s_own[:, p * HD :], -1e30)
        last_oth = jnp.where(core == 1, s_oth[:, p * HD :], -1e30)
        if p:
            s_own = jnp.concatenate([s_own[:, : p * HD], last_own], axis=1)
            s_oth = jnp.concatenate([s_oth[:, : p * HD], last_oth], axis=1)
        else:
            s_own, s_oth = last_own, last_oth
        top = jnp.maximum(
            jnp.max(s_own, axis=-1, keepdims=True), jnp.max(s_oth, axis=-1, keepdims=True)
        )
        e_own = jnp.exp(s_own - top)
        e_oth = jnp.exp(s_oth - top)
        total = jnp.sum(e_own, axis=-1, keepdims=True) + jnp.sum(e_oth, axis=-1, keepdims=True)
        acc = jnp.dot(e_own.astype(jnp.bfloat16), v_own, preferred_element_type=jnp.float32)
        acc += jnp.dot(e_oth.astype(jnp.bfloat16), v_oth, preferred_element_type=jnp.float32)
        out_ref[p] = (acc / total).astype(jnp.bfloat16)


def attend(core, own, other):
    count = own.shape[0]
    return pl.pallas_call(
        attend_kernel,
        out_shape=jax.ShapeDtypeStruct((count, HD, HD), jnp.bfloat16),
        in_specs=[
            pl.BlockSpec(memory_space=pltpu.SMEM),
            pl.BlockSpec(memory_space=pltpu.VMEM),
            pl.BlockSpec(memory_space=pltpu.VMEM),
        ],
        out_specs=pl.BlockSpec(memory_space=pltpu.VMEM),
        compiler_params=pltpu.CompilerParams(vmem_limit_bytes=16 * 2**20),
        cost_estimate=pl.CostEstimate(
            flops=700_000_000, bytes_accessed=1_600_000, transcendentals=1_200_000
        ),
    )(core, own, other)


def project_kernel(att_ref, weight_ref, input_ref, gain_ref, res_ref, normed_ref, w_vmem, sems):
    heads = att_ref.shape[0]
    width = weight_ref.shape[1]
    tile = w_vmem.shape[2]
    tiles = width // tile
    copies = [
        pltpu.make_async_copy(
            weight_ref.at[:, pl.ds(j * tile, tile)], w_vmem.at[j], sems.at[j]
        )
        for j in range(tiles)
    ]
    for copy in copies:
        copy.start()
    att = jnp.concatenate([att_ref[h] for h in range(heads)], axis=1)
    square = jnp.zeros((att.shape[0], 1), jnp.float32)
    for j in range(tiles):
        cols = slice(j * tile, (j + 1) * tile)
        copies[j].wait()
        part = jnp.dot(att, w_vmem[j], preferred_element_type=jnp.float32)
        part = (part + input_ref[:, cols].astype(jnp.float32)).astype(jnp.bfloat16)
        res_ref[:, cols] = part
        part = part.astype(jnp.float32)
        square += jnp.sum(part * part, axis=-1, keepdims=True)
    factor = lax.rsqrt(square / width + 1e-06)
    for j in range(tiles):
        cols = slice(j * tile, (j + 1) * tile)
        normed_ref[:, cols] = (
            res_ref[:, cols].astype(jnp.float32) * factor * gain_ref[:, cols]
        ).astype(jnp.bfloat16)


def project(att, weight, layer_input, gain):
    rows, width = layer_input.shape
    vmem = pl.BlockSpec(memory_space=pltpu.VMEM)
    tile = 512
    return pl.pallas_call(
        project_kernel,
        out_shape=(jax.ShapeDtypeStruct((rows, width), jnp.bfloat16),) * 2,
        in_specs=[vmem, pl.BlockSpec(memory_space=pltpu.HBM), vmem, vmem],
        out_specs=(vmem, vmem),
        scratch_shapes=[
            pltpu.VMEM((width // tile, weight.shape[0], tile), jnp.bfloat16),
            pltpu.SemaphoreType.DMA((width // tile,)),
        ],
        compiler_params=pltpu.CompilerParams(vmem_limit_bytes=60 * 2**20),
        cost_estimate=pl.CostEstimate(
            flops=540_000_000, bytes_accessed=6_000_000, transcendentals=128
        ),
    )(att, weight, layer_input, gain)


def pick_kernel(group, placing_ref, *refs):
    count = len(group)
    block_refs, (own_ref, core_ref, side_ref, held, sems) = refs[:count], refs[count:]
    width = own_ref.shape[1]
    size = count * SLOT
    copies = [
        pltpu.make_async_copy(block_refs[i], held.at[i], sems.at[i]) for i in range(count)
    ]
    for copy in copies:
        copy.start()
    tile = 512
    for i, d in enumerate(group):
        copies[i].wait()
        for j in range(width // tile):
            cols = slice(j * tile, (j + 1) * tile)
            rows = jnp.dot(placing_ref[d], held[i, :, cols], preferred_element_type=jnp.float32)
            rows = rows.astype(jnp.bfloat16)
            at = i * SLOT
            own_ref[at : at + SLOT, cols] = rows[:SLOT]
            core_ref[at : at + SLOT, cols] = rows[SLOT : 2 * SLOT]
            side_ref[at : at + SLOT, cols] = rows[2 * SLOT : 3 * SLOT]
            side_ref[size + at : size + at + SLOT, cols] = rows[3 * SLOT :]


def pick(group, placing, blocks):
    tok, width = blocks[0].shape
    vmem = pl.BlockSpec(memory_space=pltpu.VMEM)
    rows = len(group) * SLOT
    return pl.pallas_call(
        functools.partial(pick_kernel, group),
        out_shape=[jax.ShapeDtypeStruct((k * rows, width), jnp.bfloat16) for k in (1, 1, 2)],
        in_specs=[vmem] + [pl.BlockSpec(memory_space=pltpu.HBM)] * len(blocks),
        out_specs=[vmem] * 3,
        scratch_shapes=[
            pltpu.VMEM((len(blocks), tok, width), jnp.bfloat16),
            pltpu.SemaphoreType.DMA((len(blocks),)),
        ],
        compiler_params=pltpu.CompilerParams(vmem_limit_bytes=60 * 2**20),
        cost_estimate=pl.CostEstimate(
            flops=2 * 4 * rows * HD * width, bytes_accessed=16 * rows * width, transcendentals=0
        ),
    )(placing, *blocks)


def expert_kernel(spans, place_ref, *refs):
    count = len(spans)
    x_refs, w_refs, out_refs = refs[:count], refs[count : -5 - count], refs[-5 - count : -5]
    w_vmem, x_all, acc_ref, hid_ref, sems = refs[-5:]
    pieces = len(w_refs)
    depth = w_refs[0].shape[0]
    copies = [
        pltpu.make_async_copy(w_refs[j], w_vmem.at[j], sems.at[j]) for j in range(pieces)
    ]
    for copy in copies:
        copy.start()
    for x_ref, (at, size) in zip(x_refs, spans):
        x_all[at : at + size] = x_ref[...]
    both = acc_ref.shape[1]
    ffe = both // 2
    hid_ref[...] = jnp.zeros_like(hid_ref)
    for j in range(pieces):
        copies[j].wait()
        cols = pl.ds(pl.multiple_of(place_ref[j] * depth, depth), depth)
        part = jnp.dot(x_all[:, cols], w_vmem[j, :, :both], preferred_element_type=jnp.float32)
        if j == 0:
            acc_ref[...] = part
        else:
            acc_ref[...] += part
    gate = acc_ref[:, :ffe]
    up = acc_ref[:, ffe:]
    hid_ref[:, :ffe] = (gate / (1.0 + jnp.exp(-gate)) * up).astype(jnp.bfloat16)
    hid = hid_ref[...]
    for j in range(pieces):
        cols = pl.ds(pl.multiple_of(place_ref[j] * depth, depth), depth)
        made = lax.dot_general(
            hid, w_vmem[j, :, both:], (((1,), (1,)), ((), ())), preferred_element_type=jnp.float32
        ).astype(jnp.bfloat16)
        for out_ref, (at, size) in zip(out_refs, spans):
            out_ref[:, cols] = made[at : at + size]


def expert(places, x, pieces, ffe):
    width = x[0].shape[1]
    depth, lanes = pieces[0].shape
    spans, total = [], 0
    for a in x:
        spans.append((total, a.shape[0]))
        total += a.shape[0]
    vmem = pl.BlockSpec(memory_space=pltpu.VMEM)
    return pl.pallas_call(
        functools.partial(expert_kernel, tuple(spans)),
        out_shape=[jax.ShapeDtypeStruct(a.shape, jnp.bfloat16) for a in x],
        in_specs=[pl.BlockSpec(memory_space=pltpu.SMEM)]
        + [vmem] * len(x)
        + [pl.BlockSpec(memory_space=pltpu.HBM)] * len(pieces),
        out_specs=[vmem] * len(x),
        scratch_shapes=[
            pltpu.VMEM((len(pieces), depth, lanes), jnp.bfloat16),
            pltpu.VMEM((total, width), jnp.bfloat16),
            pltpu.VMEM((total, 2 * ffe), jnp.float32),
            pltpu.VMEM((total, lanes - 2 * ffe), jnp.bfloat16),
            pltpu.SemaphoreType.DMA((len(pieces),)),
        ],
        compiler_params=pltpu.CompilerParams(vmem_limit_bytes=60 * 2**20),
        cost_estimate=pl.CostEstimate(
            flops=6 * total * width * ffe,
            bytes_accessed=6 * width * ffe + 4 * total * width,
            transcendentals=total * ffe,
        ),
    )(places, *x, *pieces)


def body(
    layer_input,
    queries,
    keys,
    values,
    out_weight,
    norm_gain,
    route_ids,
    route_weight,
    w_gate,
    w_up,
    w_down,
):
    tok = layer_input.shape[1]
    ctx = lax.axis_index("ctx")
    exp = lax.axis_index("exp")
    core, y, xh = ctx % 2, ctx // 2 % NY, ctx // (2 * NY)
    z, xl = exp // 2, exp % 2
    same_core = [[p * 2 + c for p in range(2 * NY)] for c in range(2)]

    ffe = w_gate.shape[2]
    lanes = -(-3 * ffe // HD) * HD
    down_rows = jnp.swapaxes(w_down, 1, 2)
    blank = jnp.zeros((w_gate.shape[1], lanes - 3 * ffe), w_gate.dtype)

    def local(e):
        return jnp.concatenate([w_gate[e], w_up[e], down_rows[e], blank], axis=1)

    first = core == 0
    zero, one = local(0), local(1)
    come = ctx_shift(jnp.where(first, one, zero), 0, 0, 1)
    piece = jnp.concatenate(
        [jnp.where(first, zero, come), jnp.where(first, come, one)], axis=0
    )
    far = ctx_shift(piece, 1, 0, 0)
    near_up, near_down = ctx_shift(piece, 0, 1, 0), ctx_shift(piece, 0, -1, 0)

    picks = jnp.concatenate([route_ids[0].T.astype(jnp.float32), route_weight[0].T], axis=0)
    picks = picks[None]
    picks = jnp.concatenate([picks, z_shift(picks, 1)], axis=0)

    heads = jnp.stack([queries[0], keys[0], values[0]]).reshape(3, tok, -1, HD)
    heads = heads.transpose(2, 0, 1, 3)
    own = lax.all_to_all(heads, "ctx", 0, 0, axis_index_groups=same_core, tiled=True)
    own, picks = lax.optimization_barrier((own, picks))
    other = ctx_shift(own, 0, 0, 1)
    picks = jnp.concatenate([picks, z_shift(picks, 2)], axis=0)
    attended = attend(core.reshape(1), own, other)
    attended, picks = lax.optimization_barrier((attended, picks))
    picks = jnp.concatenate([picks, z_shift(picks, 4)], axis=0)
    attended = lax.all_to_all(attended, "ctx", 0, 0, axis_index_groups=same_core, tiled=True)
    attended, picks, far, near_up, near_down = lax.optimization_barrier(
        (attended, picks, far, near_up, near_down)
    )
    far_up, far_down = ctx_shift(far, 0, 1, 0), ctx_shift(far, 0, -1, 0)

    top = route_ids.shape[2]
    ids, weights = picks[:, :top], picks[:, top:]
    quarter = jnp.arange(4)
    wanted = (4 * z + ((2 * xl + core) ^ quarter)).astype(jnp.float32)
    hits = ids[:, None] == wanted[None, :, None, None]
    hit = jnp.sum(hits.astype(jnp.float32), axis=2)
    share = jnp.sum(jnp.where(hits, weights[:, None], 0.0), axis=2)
    before = (jnp.arange(tok)[:, None] < jnp.arange(tok)[None, :]).astype(jnp.bfloat16)
    rank = jnp.einsum(
        "drs,st->drt", hit.astype(jnp.bfloat16), before, preferred_element_type=jnp.float32
    )
    slots = jnp.arange(SLOT, dtype=jnp.float32)
    at_slot = rank[:, :, None, :] == slots[None, None, :, None]
    placing = jnp.where(at_slot, hit[:, :, None, :], 0.0).reshape(NZ, 4 * SLOT, tok)
    placing = placing.astype(jnp.bfloat16)
    merging = jnp.where(at_slot, share[:, :, None, :], 0.0).reshape(NZ, 4 * SLOT, tok)
    merging = merging.transpose(0, 2, 1).astype(jnp.bfloat16)

    residual, normed = project(attended, out_weight, layer_input[0], norm_gain[None])

    swaps = (lambda a: a, lambda a: ctx_shift(a, 0, 0, 1), x_swap, diag_swap)

    half = tok // 2
    blocks = {0: normed}
    for d in (1, 2, 3):
        blocks[d] = z_shift(blocks[d - 1], 1)
        blocks[NZ - d] = z_shift(blocks[(NZ - d + 1) % NZ], -1)
    blocks[4] = jnp.concatenate(
        [z_shift(blocks[3][:half], 1), z_shift(blocks[5][half:], -1)], axis=0
    )
    inputs = [[blocks[d] for d in group] for group in GROUPS]
    sizes = [len(group) * SLOT for group in GROUPS]
    own, cross, side = {}, {}, {}

    def send(g):
        own[g], cross[g], leaving = pick(GROUPS[g], placing, inputs[g])
        side[g] = x_swap(leaving)

    def over_cores(groups, a, b):
        both = swaps[1](jnp.concatenate([a[g] for g in groups] + [b[g] for g in groups], axis=0))
        out, at = [], 0
        for _ in range(2):
            parts = {}
            for g in groups:
                parts[g] = both[at : at + sizes[g]]
                at += sizes[g]
            out.append(parts)
        return out

    send(0)
    inputs[1], side[0], far_up, far_down = lax.optimization_barrier(
        (inputs[1], side[0], far_up, far_down)
    )
    near_two, far_two = ctx_shift(near_up, 0, 1, 0), ctx_shift(far_down, 0, -1, 0)
    send(1)
    inputs[2], side[1], near_two, far_two = lax.optimization_barrier(
        (inputs[2], side[1], near_two, far_two)
    )
    spots = ((0, 0), (1, 0), (0, -1), (0, 1), (1, -1), (1, 1), (0, 2), (1, 2))
    pieces = [piece, far, near_up, near_down, far_up, far_down, near_two, far_two]
    places = jnp.stack([(xh + dx) % 2 * NY + (y + dy) % NY for dx, dy in spots])

    def halves_of(g):
        return side[g][: sizes[g]], side[g][sizes[g] :]

    straight, slant = {}, {}
    for g in (0, 1):
        straight[g], slant[g] = halves_of(g)
    core_rows, far_rows = over_cores((0, 1), cross, slant)

    def send_straight(g, rows):
        return [rows[0], swaps[1](rows[1]), x_swap(rows[2][: sizes[g]]), diag_swap(rows[2][sizes[g] :])]

    middle = send_straight(2, pick(GROUPS[2], placing, inputs[2]))
    last = pick(GROUPS[3], placing, inputs[3])
    core_rows, last = lax.optimization_barrier((core_rows, last))
    final = send_straight(3, last)
    early = expert(
        places,
        [kind[g] for kind in (own, straight, core_rows, far_rows) for g in (0, 1)],
        pieces,
        ffe,
    )
    early, middle, final = lax.optimization_barrier((early, middle, final))
    own[0], own[1], straight[0], straight[1] = early[:4]
    core_back, far_back = over_cores((0, 1), early[4:6], early[6:])

    def side_back(g):
        back = x_swap(jnp.concatenate([straight[g], far_back[g]], axis=0))
        return [own[g], core_back[g], back[: sizes[g]], back[sizes[g] :]]

    final = expert(places, final, pieces, ffe)
    final = [swaps[r](final[r]) for r in range(4)]
    middle = expert(places, middle, pieces, ffe)
    done = {1: side_back(1)}
    final, middle, done[1] = lax.optimization_barrier((final, middle, done[1]))
    middle = [swaps[r](middle[r]) for r in range(4)]
    done |= {3: final, 2: middle, 0: side_back(0)}

    def returned(d):
        g = next(i for i, group in enumerate(GROUPS) if d in group)
        i = GROUPS[g].index(d)
        return jnp.concatenate([a[i * SLOT : (i + 1) * SLOT] for a in done[g]], axis=0)

    def part(d, h):
        return jnp.dot(
            merging[d, h * half : (h + 1) * half], returned(d), preferred_element_type=jnp.float32
        )

    def narrow(a):
        return a.astype(jnp.bfloat16)

    def wide(a):
        return a.astype(jnp.float32)

    up = [z_shift(narrow(part(4, 0)), 1), None]
    down = [None, z_shift(narrow(part(4, 1)), -1)]
    for d in (3, 2, 1):
        for h in range(2):
            more = part(NZ - d, h)
            up[h] = z_shift(narrow(more if up[h] is None else more + wide(up[h])), 1)
            more = part(d, 1 - h)
            kept = down[1 - h]
            down[1 - h] = z_shift(narrow(more if kept is None else more + wide(kept)), -1)
        if d == 3:
            up, down, done[0] = lax.optimization_barrier((up, down, done[0]))
    mixed = [
        narrow(wide(residual[h * half : (h + 1) * half]) + part(0, h) + wide(up[h]) + wide(down[h]))
        for h in range(2)
    ]
    return jnp.concatenate(mixed, axis=0)[None]


def solution(mesh):
    return jax.shard_map(
        body,
        mesh=mesh,
        in_specs=(
            P("exp", "ctx", None),
            P("exp", "ctx", None),
            P("exp", "ctx", None),
            P("exp", "ctx", None),
            P(),
            P(),
            P("exp", "ctx", None),
            P("exp", "ctx", None),
            P("exp", "ctx", None),
            P("exp", "ctx", None),
            P("exp", None, "ctx"),
        ),
        out_specs=P("exp", "ctx", None),
        check_vma=False,
    )
```

```python
import functools
import math

import jax
import jax.numpy as jnp
from jax import lax
from jax.experimental import pallas as pl
from jax.experimental.pallas import tpu as pltpu
from jax.sharding import PartitionSpec as P

HD = 128
SLOT = 32
NY = 4
NZ = 8
GROUPS = ((0, 1, 7), (2, 6), (3, 5), (4,))


def ctx_pairs(dx, dy, dc):
    pairs = []
    for i in range(16):
        xh, y, c = i // 8, i // 2 % NY, i % 2
        pairs.append((i, ((xh + dx) % 2 * NY + (y + dy) % NY) * 2 + (c + dc) % 2))
    return pairs


def z_pairs(d):
    return [(z * 2 + x, (z + d) % NZ * 2 + x) for z in range(NZ) for x in range(2)]


def ctx_shift(a, dx, dy, dc):
    return lax.ppermute(a, "ctx", ctx_pairs(dx, dy, dc))


def z_shift(a, d):
    return lax.ppermute(a, "exp", z_pairs(d))


def x_swap(a):
    return lax.ppermute(a, "exp", [(i, i ^ 1) for i in range(16)])


def diag_swap(a):
    pairs = [(c * 16 + e, (c ^ 1) * 16 + (e ^ 1)) for c in range(16) for e in range(16)]
    return lax.ppermute(a, ("ctx", "exp"), pairs)


def attend_kernel(core_ref, own_ref, other_ref, out_ref):
    count = own_ref.shape[0]
    core = core_ref[0]
    row = lax.broadcasted_iota(jnp.int32, (HD, HD), 0)
    col = lax.broadcasted_iota(jnp.int32, (HD, HD), 1)
    dims = (((1,), (1,)), ((), ()))
    scale = 1.0 / math.sqrt(HD)
    for p in range(count):
        q = own_ref[p, 0]
        width = (p + 1) * HD
        k_own = own_ref[: p + 1, 1].reshape(width, HD)
        v_own = own_ref[: p + 1, 2].reshape(width, HD)
        k_oth = other_ref[: p + 1, 1].reshape(width, HD)
        v_oth = other_ref[: p + 1, 2].reshape(width, HD)
        s_own = lax.dot_general(q, k_own, dims, preferred_element_type=jnp.float32) * scale
        s_oth = lax.dot_general(q, k_oth, dims, preferred_element_type=jnp.float32) * scale
        last_own = jnp.where(row >= col, s_own[:, p * HD :], -1e30)
        last_oth = jnp.where(core == 1, s_oth[:, p * HD :], -1e30)
        if p:
            s_own = jnp.concatenate([s_own[:, : p * HD], last_own], axis=1)
            s_oth = jnp.concatenate([s_oth[:, : p * HD], last_oth], axis=1)
        else:
            s_own, s_oth = last_own, last_oth
        top = jnp.maximum(
            jnp.max(s_own, axis=-1, keepdims=True), jnp.max(s_oth, axis=-1, keepdims=True)
        )
        e_own = jnp.exp(s_own - top)
        e_oth = jnp.exp(s_oth - top)
        total = jnp.sum(e_own, axis=-1, keepdims=True) + jnp.sum(e_oth, axis=-1, keepdims=True)
        acc = jnp.dot(e_own.astype(jnp.bfloat16), v_own, preferred_element_type=jnp.float32)
        acc += jnp.dot(e_oth.astype(jnp.bfloat16), v_oth, preferred_element_type=jnp.float32)
        out_ref[p] = (acc / total).astype(jnp.bfloat16)


def attend(core, own, other):
    count = own.shape[0]
    return pl.pallas_call(
        attend_kernel,
        out_shape=jax.ShapeDtypeStruct((count, HD, HD), jnp.bfloat16),
        in_specs=[
            pl.BlockSpec(memory_space=pltpu.SMEM),
            pl.BlockSpec(memory_space=pltpu.VMEM),
            pl.BlockSpec(memory_space=pltpu.VMEM),
        ],
        out_specs=pl.BlockSpec(memory_space=pltpu.VMEM),
        compiler_params=pltpu.CompilerParams(vmem_limit_bytes=16 * 2**20),
        cost_estimate=pl.CostEstimate(
            flops=700_000_000, bytes_accessed=1_600_000, transcendentals=1_200_000
        ),
    )(core, own, other)


def project_kernel(att_ref, weight_ref, input_ref, gain_ref, res_ref, normed_ref, w_vmem, sems):
    heads = att_ref.shape[0]
    width = weight_ref.shape[1]
    tile = w_vmem.shape[2]
    tiles = width // tile
    copies = [
        pltpu.make_async_copy(
            weight_ref.at[:, pl.ds(j * tile, tile)], w_vmem.at[j], sems.at[j]
        )
        for j in range(tiles)
    ]
    for copy in copies:
        copy.start()
    att = jnp.concatenate([att_ref[h] for h in range(heads)], axis=1)
    square = jnp.zeros((att.shape[0], 1), jnp.float32)
    for j in range(tiles):
        cols = slice(j * tile, (j + 1) * tile)
        copies[j].wait()
        part = jnp.dot(att, w_vmem[j], preferred_element_type=jnp.float32)
        part = (part + input_ref[:, cols].astype(jnp.float32)).astype(jnp.bfloat16)
        res_ref[:, cols] = part
        part = part.astype(jnp.float32)
        square += jnp.sum(part * part, axis=-1, keepdims=True)
    factor = lax.rsqrt(square / width + 1e-06)
    for j in range(tiles):
        cols = slice(j * tile, (j + 1) * tile)
        normed_ref[:, cols] = (
            res_ref[:, cols].astype(jnp.float32) * factor * gain_ref[:, cols]
        ).astype(jnp.bfloat16)


def project(att, weight, layer_input, gain):
    rows, width = layer_input.shape
    vmem = pl.BlockSpec(memory_space=pltpu.VMEM)
    tile = 512
    return pl.pallas_call(
        project_kernel,
        out_shape=(jax.ShapeDtypeStruct((rows, width), jnp.bfloat16),) * 2,
        in_specs=[vmem, pl.BlockSpec(memory_space=pltpu.HBM), vmem, vmem],
        out_specs=(vmem, vmem),
        scratch_shapes=[
            pltpu.VMEM((width // tile, weight.shape[0], tile), jnp.bfloat16),
            pltpu.SemaphoreType.DMA((width // tile,)),
        ],
        compiler_params=pltpu.CompilerParams(vmem_limit_bytes=60 * 2**20),
        cost_estimate=pl.CostEstimate(
            flops=540_000_000, bytes_accessed=6_000_000, transcendentals=128
        ),
    )(att, weight, layer_input, gain)


def pick_kernel(group, placing_ref, *refs):
    count = len(group)
    block_refs, (own_ref, core_ref, side_ref, held, sems) = refs[:count], refs[count:]
    width = own_ref.shape[1]
    size = count * SLOT
    copies = [
        pltpu.make_async_copy(block_refs[i], held.at[i], sems.at[i]) for i in range(count)
    ]
    for copy in copies:
        copy.start()
    tile = 512
    for i, d in enumerate(group):
        copies[i].wait()
        for j in range(width // tile):
            cols = slice(j * tile, (j + 1) * tile)
            rows = jnp.dot(placing_ref[d], held[i, :, cols], preferred_element_type=jnp.float32)
            rows = rows.astype(jnp.bfloat16)
            at = i * SLOT
            own_ref[at : at + SLOT, cols] = rows[:SLOT]
            core_ref[at : at + SLOT, cols] = rows[SLOT : 2 * SLOT]
            side_ref[at : at + SLOT, cols] = rows[2 * SLOT : 3 * SLOT]
            side_ref[size + at : size + at + SLOT, cols] = rows[3 * SLOT :]


def pick(group, placing, blocks):
    tok, width = blocks[0].shape
    vmem = pl.BlockSpec(memory_space=pltpu.VMEM)
    rows = len(group) * SLOT
    return pl.pallas_call(
        functools.partial(pick_kernel, group),
        out_shape=[jax.ShapeDtypeStruct((k * rows, width), jnp.bfloat16) for k in (1, 1, 2)],
        in_specs=[vmem] + [pl.BlockSpec(memory_space=pltpu.HBM)] * len(blocks),
        out_specs=[vmem] * 3,
        scratch_shapes=[
            pltpu.VMEM((len(blocks), tok, width), jnp.bfloat16),
            pltpu.SemaphoreType.DMA((len(blocks),)),
        ],
        compiler_params=pltpu.CompilerParams(vmem_limit_bytes=60 * 2**20),
        cost_estimate=pl.CostEstimate(
            flops=2 * 4 * rows * HD * width, bytes_accessed=16 * rows * width, transcendentals=0
        ),
    )(placing, *blocks)


def expert_kernel(spans, place_ref, *refs):
    count = len(spans)
    x_refs, w_refs, out_refs = refs[:count], refs[count : -5 - count], refs[-5 - count : -5]
    w_vmem, x_all, acc_ref, hid_ref, sems = refs[-5:]
    pieces = len(w_refs)
    depth = w_refs[0].shape[0]
    copies = [
        pltpu.make_async_copy(w_refs[j], w_vmem.at[j], sems.at[j]) for j in range(pieces)
    ]
    for copy in copies:
        copy.start()
    for x_ref, (at, size) in zip(x_refs, spans):
        x_all[at : at + size] = x_ref[...]
    both = acc_ref.shape[1]
    ffe = both // 2
    hid_ref[...] = jnp.zeros_like(hid_ref)
    for j in range(pieces):
        copies[j].wait()
        cols = pl.ds(pl.multiple_of(place_ref[j] * depth, depth), depth)
        part = jnp.dot(x_all[:, cols], w_vmem[j, :, :both], preferred_element_type=jnp.float32)
        if j == 0:
            acc_ref[...] = part
        else:
            acc_ref[...] += part
    gate = acc_ref[:, :ffe]
    up = acc_ref[:, ffe:]
    hid_ref[:, :ffe] = (gate / (1.0 + jnp.exp(-gate)) * up).astype(jnp.bfloat16)
    hid = hid_ref[...]
    for j in range(pieces):
        cols = pl.ds(pl.multiple_of(place_ref[j] * depth, depth), depth)
        made = lax.dot_general(
            hid, w_vmem[j, :, both:], (((1,), (1,)), ((), ())), preferred_element_type=jnp.float32
        ).astype(jnp.bfloat16)
        for out_ref, (at, size) in zip(out_refs, spans):
            out_ref[:, cols] = made[at : at + size]


def expert(places, x, pieces, ffe):
    width = x[0].shape[1]
    depth, lanes = pieces[0].shape
    spans, total = [], 0
    for a in x:
        spans.append((total, a.shape[0]))
        total += a.shape[0]
    vmem = pl.BlockSpec(memory_space=pltpu.VMEM)
    return pl.pallas_call(
        functools.partial(expert_kernel, tuple(spans)),
        out_shape=[jax.ShapeDtypeStruct(a.shape, jnp.bfloat16) for a in x],
        in_specs=[pl.BlockSpec(memory_space=pltpu.SMEM)]
        + [vmem] * len(x)
        + [pl.BlockSpec(memory_space=pltpu.HBM)] * len(pieces),
        out_specs=[vmem] * len(x),
        scratch_shapes=[
            pltpu.VMEM((len(pieces), depth, lanes), jnp.bfloat16),
            pltpu.VMEM((total, width), jnp.bfloat16),
            pltpu.VMEM((total, 2 * ffe), jnp.float32),
            pltpu.VMEM((total, lanes - 2 * ffe), jnp.bfloat16),
            pltpu.SemaphoreType.DMA((len(pieces),)),
        ],
        compiler_params=pltpu.CompilerParams(vmem_limit_bytes=60 * 2**20),
        cost_estimate=pl.CostEstimate(
            flops=6 * total * width * ffe,
            bytes_accessed=6 * width * ffe + 4 * total * width,
            transcendentals=total * ffe,
        ),
    )(places, *x, *pieces)


def body(
    layer_input,
    queries,
    keys,
    values,
    out_weight,
    norm_gain,
    route_ids,
    route_weight,
    w_gate,
    w_up,
    w_down,
):
    tok = layer_input.shape[1]
    ctx = lax.axis_index("ctx")
    exp = lax.axis_index("exp")
    core, y, xh = ctx % 2, ctx // 2 % NY, ctx // (2 * NY)
    z, xl = exp // 2, exp % 2
    same_core = [[p * 2 + c for p in range(2 * NY)] for c in range(2)]

    ffe = w_gate.shape[2]
    lanes = -(-3 * ffe // HD) * HD
    down_rows = jnp.swapaxes(w_down, 1, 2)
    blank = jnp.zeros((w_gate.shape[1], lanes - 3 * ffe), w_gate.dtype)

    def local(e):
        return jnp.concatenate([w_gate[e], w_up[e], down_rows[e], blank], axis=1)

    first = core == 0
    zero, one = local(0), local(1)
    come = ctx_shift(jnp.where(first, one, zero), 0, 0, 1)
    piece = jnp.concatenate(
        [jnp.where(first, zero, come), jnp.where(first, come, one)], axis=0
    )
    far = ctx_shift(piece, 1, 0, 0)
    near_up, near_down = ctx_shift(piece, 0, 1, 0), ctx_shift(piece, 0, -1, 0)

    picks = jnp.concatenate([route_ids[0].T.astype(jnp.float32), route_weight[0].T], axis=0)
    picks = picks[None]
    picks = jnp.concatenate([picks, z_shift(picks, 1)], axis=0)

    heads = jnp.stack([queries[0], keys[0], values[0]]).reshape(3, tok, -1, HD)
    heads = heads.transpose(2, 0, 1, 3)
    own = lax.all_to_all(heads, "ctx", 0, 0, axis_index_groups=same_core, tiled=True)
    own, picks = lax.optimization_barrier((own, picks))
    other = ctx_shift(own, 0, 0, 1)
    picks = jnp.concatenate([picks, z_shift(picks, 2)], axis=0)
    attended = attend(core.reshape(1), own, other)
    attended, picks = lax.optimization_barrier((attended, picks))
    picks = jnp.concatenate([picks, z_shift(picks, 4)], axis=0)
    attended = lax.all_to_all(attended, "ctx", 0, 0, axis_index_groups=same_core, tiled=True)
    attended, picks, far, near_up, near_down = lax.optimization_barrier(
        (attended, picks, far, near_up, near_down)
    )
    near_two, far_down = ctx_shift(near_up, 0, 1, 0), ctx_shift(far, 0, -1, 0)

    top = route_ids.shape[2]
    ids, weights = picks[:, :top], picks[:, top:]
    quarter = jnp.arange(4)
    wanted = (4 * z + ((2 * xl + core) ^ quarter)).astype(jnp.float32)
    hits = ids[:, None] == wanted[None, :, None, None]
    hit = jnp.sum(hits.astype(jnp.float32), axis=2)
    share = jnp.sum(jnp.where(hits, weights[:, None], 0.0), axis=2)
    before = (jnp.arange(tok)[:, None] < jnp.arange(tok)[None, :]).astype(jnp.bfloat16)
    rank = jnp.einsum(
        "drs,st->drt", hit.astype(jnp.bfloat16), before, preferred_element_type=jnp.float32
    )
    slots = jnp.arange(SLOT, dtype=jnp.float32)
    at_slot = rank[:, :, None, :] == slots[None, None, :, None]
    placing = jnp.where(at_slot, hit[:, :, None, :], 0.0).reshape(NZ, 4 * SLOT, tok)
    placing = placing.astype(jnp.bfloat16)
    merging = jnp.where(at_slot, share[:, :, None, :], 0.0).reshape(NZ, 4 * SLOT, tok)
    merging = merging.transpose(0, 2, 1).astype(jnp.bfloat16)

    residual, normed = project(attended, out_weight, layer_input[0], norm_gain[None])

    swaps = (lambda a: a, lambda a: ctx_shift(a, 0, 0, 1), x_swap, diag_swap)

    half = tok // 2
    blocks = {0: normed}
    for d in (1, 2, 3):
        blocks[d] = z_shift(blocks[d - 1], 1)
        blocks[NZ - d] = z_shift(blocks[(NZ - d + 1) % NZ], -1)
    blocks[4] = jnp.concatenate(
        [z_shift(blocks[3][:half], 1), z_shift(blocks[5][half:], -1)], axis=0
    )
    inputs = [[blocks[d] for d in group] for group in GROUPS]
    sizes = [len(group) * SLOT for group in GROUPS]
    own, cross, side = {}, {}, {}

    def send(g):
        own[g], cross[g], leaving = pick(GROUPS[g], placing, inputs[g])
        side[g] = x_swap(leaving)

    def over_cores(groups, a, b):
        both = swaps[1](jnp.concatenate([a[g] for g in groups] + [b[g] for g in groups], axis=0))
        out, at = [], 0
        for _ in range(2):
            parts = {}
            for g in groups:
                parts[g] = both[at : at + sizes[g]]
                at += sizes[g]
            out.append(parts)
        return out

    inputs[0], near_two, far_down = lax.optimization_barrier((inputs[0], near_two, far_down))
    far_up, far_two = ctx_shift(far, 0, 1, 0), ctx_shift(far_down, 0, -1, 0)
    send(0)
    inputs[1], side[0], far_up, far_two = lax.optimization_barrier(
        (inputs[1], side[0], far_up, far_two)
    )
    send(1)
    inputs[2], side[1] = lax.optimization_barrier((inputs[2], side[1]))
    spots = ((0, 0), (1, 0), (0, -1), (0, 1), (1, -1), (1, 1), (0, 2), (1, 2))
    pieces = [piece, far, near_up, near_down, far_up, far_down, near_two, far_two]
    places = jnp.stack([(xh + dx) % 2 * NY + (y + dy) % NY for dx, dy in spots])

    def halves_of(g):
        return side[g][: sizes[g]], side[g][sizes[g] :]

    straight, slant = {}, {}
    for g in (0, 1):
        straight[g], slant[g] = halves_of(g)
    core_rows, far_rows = over_cores((0, 1), cross, slant)

    def send_straight(g, rows):
        return [rows[0], swaps[1](rows[1]), x_swap(rows[2][: sizes[g]]), diag_swap(rows[2][sizes[g] :])]

    middle = send_straight(2, pick(GROUPS[2], placing, inputs[2]))
    last = pick(GROUPS[3], placing, inputs[3])
    core_rows, last = lax.optimization_barrier((core_rows, last))
    final = send_straight(3, last)
    early = expert(
        places,
        [kind[g] for kind in (own, straight, core_rows, far_rows) for g in (0, 1)],
        pieces,
        ffe,
    )
    early, middle, final = lax.optimization_barrier((early, middle, final))

    def send_back(rows):
        own_rows, beside, core_rows, far_rows = rows
        return [own_rows, swaps[1](core_rows), x_swap(beside), diag_swap(far_rows)]

    final = expert(places, final, pieces, ffe)
    final = [swaps[r](final[r]) for r in range(4)]
    middle = expert(places, middle, pieces, ffe)
    final, middle = lax.optimization_barrier((final, middle))
    done = {3: final, 2: [swaps[r](middle[r]) for r in range(4)]}
    done |= {1: send_back(early[1::2]), 0: send_back(early[0::2])}

    def returned(d):
        g = next(i for i, group in enumerate(GROUPS) if d in group)
        i = GROUPS[g].index(d)
        return jnp.concatenate([a[i * SLOT : (i + 1) * SLOT] for a in done[g]], axis=0)

    def part(d, h):
        return jnp.dot(
            merging[d, h * half : (h + 1) * half], returned(d), preferred_element_type=jnp.float32
        )

    def narrow(a):
        return a.astype(jnp.bfloat16)

    def wide(a):
        return a.astype(jnp.float32)

    up = [z_shift(narrow(part(4, 0)), 1), None]
    down = [None, z_shift(narrow(part(4, 1)), -1)]
    up, down, done[2], done[1] = lax.optimization_barrier((up, down, done[2], done[1]))
    for d in (3, 2, 1):
        for h in range(2):
            more = part(NZ - d, h)
            up[h] = z_shift(narrow(more if up[h] is None else more + wide(up[h])), 1)
            more = part(d, 1 - h)
            kept = down[1 - h]
            down[1 - h] = z_shift(narrow(more if kept is None else more + wide(kept)), -1)
        if d == 3:
            up, down, done[0] = lax.optimization_barrier((up, down, done[0]))
    mixed = [
        narrow(wide(residual[h * half : (h + 1) * half]) + part(0, h) + wide(up[h]) + wide(down[h]))
        for h in range(2)
    ]
    return jnp.concatenate(mixed, axis=0)[None]


def solution(mesh):
    return jax.shard_map(
        body,
        mesh=mesh,
        in_specs=(
            P("exp", "ctx", None),
            P("exp", "ctx", None),
            P("exp", "ctx", None),
            P("exp", "ctx", None),
            P(),
            P(),
            P("exp", "ctx", None),
            P("exp", "ctx", None),
            P("exp", "ctx", None),
            P("exp", "ctx", None),
            P("exp", None, "ctx"),
        ),
        out_specs=P("exp", "ctx", None),
        check_vma=False,
    )
```

```python
import functools
import math

import jax
import jax.numpy as jnp
from jax import lax
from jax.experimental import pallas as pl
from jax.experimental.pallas import tpu as pltpu
from jax.sharding import PartitionSpec as P

HD = 128
SLOT = 32
NY = 4
NZ = 8
GROUPS = ((0, 1, 7), (2, 6), (3, 5), (4,))


def ctx_pairs(dx, dy, dc):
    pairs = []
    for i in range(16):
        xh, y, c = i // 8, i // 2 % NY, i % 2
        pairs.append((i, ((xh + dx) % 2 * NY + (y + dy) % NY) * 2 + (c + dc) % 2))
    return pairs


def z_pairs(d):
    return [(z * 2 + x, (z + d) % NZ * 2 + x) for z in range(NZ) for x in range(2)]


def ctx_shift(a, dx, dy, dc):
    return lax.ppermute(a, "ctx", ctx_pairs(dx, dy, dc))


def z_shift(a, d):
    return lax.ppermute(a, "exp", z_pairs(d))


def x_swap(a):
    return lax.ppermute(a, "exp", [(i, i ^ 1) for i in range(16)])


def diag_swap(a):
    pairs = [(c * 16 + e, (c ^ 1) * 16 + (e ^ 1)) for c in range(16) for e in range(16)]
    return lax.ppermute(a, ("ctx", "exp"), pairs)


def attend_kernel(core_ref, own_ref, other_ref, out_ref):
    count = own_ref.shape[0]
    core = core_ref[0]
    row = lax.broadcasted_iota(jnp.int32, (HD, HD), 0)
    col = lax.broadcasted_iota(jnp.int32, (HD, HD), 1)
    dims = (((1,), (1,)), ((), ()))
    scale = 1.0 / math.sqrt(HD)
    for p in range(count):
        q = own_ref[p, 0]
        width = (p + 1) * HD
        k_own = own_ref[: p + 1, 1].reshape(width, HD)
        v_own = own_ref[: p + 1, 2].reshape(width, HD)
        k_oth = other_ref[: p + 1, 1].reshape(width, HD)
        v_oth = other_ref[: p + 1, 2].reshape(width, HD)
        s_own = lax.dot_general(q, k_own, dims, preferred_element_type=jnp.float32) * scale
        s_oth = lax.dot_general(q, k_oth, dims, preferred_element_type=jnp.float32) * scale
        last_own = jnp.where(row >= col, s_own[:, p * HD :], -1e30)
        last_oth = jnp.where(core == 1, s_oth[:, p * HD :], -1e30)
        if p:
            s_own = jnp.concatenate([s_own[:, : p * HD], last_own], axis=1)
            s_oth = jnp.concatenate([s_oth[:, : p * HD], last_oth], axis=1)
        else:
            s_own, s_oth = last_own, last_oth
        top = jnp.maximum(
            jnp.max(s_own, axis=-1, keepdims=True), jnp.max(s_oth, axis=-1, keepdims=True)
        )
        e_own = jnp.exp(s_own - top)
        e_oth = jnp.exp(s_oth - top)
        total = jnp.sum(e_own, axis=-1, keepdims=True) + jnp.sum(e_oth, axis=-1, keepdims=True)
        acc = jnp.dot(e_own.astype(jnp.bfloat16), v_own, preferred_element_type=jnp.float32)
        acc += jnp.dot(e_oth.astype(jnp.bfloat16), v_oth, preferred_element_type=jnp.float32)
        out_ref[p] = (acc / total).astype(jnp.bfloat16)


def attend(core, own, other):
    count = own.shape[0]
    return pl.pallas_call(
        attend_kernel,
        out_shape=jax.ShapeDtypeStruct((count, HD, HD), jnp.bfloat16),
        in_specs=[
            pl.BlockSpec(memory_space=pltpu.SMEM),
            pl.BlockSpec(memory_space=pltpu.VMEM),
            pl.BlockSpec(memory_space=pltpu.VMEM),
        ],
        out_specs=pl.BlockSpec(memory_space=pltpu.VMEM),
        compiler_params=pltpu.CompilerParams(vmem_limit_bytes=16 * 2**20),
        cost_estimate=pl.CostEstimate(
            flops=700_000_000, bytes_accessed=1_600_000, transcendentals=1_200_000
        ),
    )(core, own, other)


def project_kernel(att_ref, weight_ref, input_ref, gain_ref, res_ref, normed_ref, w_vmem, sems):
    heads = att_ref.shape[0]
    width = weight_ref.shape[1]
    tile = w_vmem.shape[2]
    tiles = width // tile
    copies = [
        pltpu.make_async_copy(
            weight_ref.at[:, pl.ds(j * tile, tile)], w_vmem.at[j], sems.at[j]
        )
        for j in range(tiles)
    ]
    for copy in copies:
        copy.start()
    att = jnp.concatenate([att_ref[h] for h in range(heads)], axis=1)
    square = jnp.zeros((att.shape[0], 1), jnp.float32)
    for j in range(tiles):
        cols = slice(j * tile, (j + 1) * tile)
        copies[j].wait()
        part = jnp.dot(att, w_vmem[j], preferred_element_type=jnp.float32)
        part = (part + input_ref[:, cols].astype(jnp.float32)).astype(jnp.bfloat16)
        res_ref[:, cols] = part
        part = part.astype(jnp.float32)
        square += jnp.sum(part * part, axis=-1, keepdims=True)
    factor = lax.rsqrt(square / width + 1e-06)
    for j in range(tiles):
        cols = slice(j * tile, (j + 1) * tile)
        normed_ref[:, cols] = (
            res_ref[:, cols].astype(jnp.float32) * factor * gain_ref[:, cols]
        ).astype(jnp.bfloat16)


def project(att, weight, layer_input, gain):
    rows, width = layer_input.shape
    vmem = pl.BlockSpec(memory_space=pltpu.VMEM)
    tile = 512
    return pl.pallas_call(
        project_kernel,
        out_shape=(jax.ShapeDtypeStruct((rows, width), jnp.bfloat16),) * 2,
        in_specs=[vmem, pl.BlockSpec(memory_space=pltpu.HBM), vmem, vmem],
        out_specs=(vmem, vmem),
        scratch_shapes=[
            pltpu.VMEM((width // tile, weight.shape[0], tile), jnp.bfloat16),
            pltpu.SemaphoreType.DMA((width // tile,)),
        ],
        compiler_params=pltpu.CompilerParams(vmem_limit_bytes=60 * 2**20),
        cost_estimate=pl.CostEstimate(
            flops=540_000_000, bytes_accessed=6_000_000, transcendentals=128
        ),
    )(att, weight, layer_input, gain)


def pick_kernel(group, placing_ref, *refs):
    count = len(group)
    block_refs, (own_ref, core_ref, side_ref, held, sems) = refs[:count], refs[count:]
    width = own_ref.shape[1]
    size = count * SLOT
    copies = [
        pltpu.make_async_copy(block_refs[i], held.at[i], sems.at[i]) for i in range(count)
    ]
    for copy in copies:
        copy.start()
    tile = 512
    for i, d in enumerate(group):
        copies[i].wait()
        for j in range(width // tile):
            cols = slice(j * tile, (j + 1) * tile)
            rows = jnp.dot(placing_ref[d], held[i, :, cols], preferred_element_type=jnp.float32)
            rows = rows.astype(jnp.bfloat16)
            at = i * SLOT
            own_ref[at : at + SLOT, cols] = rows[:SLOT]
            core_ref[at : at + SLOT, cols] = rows[SLOT : 2 * SLOT]
            side_ref[at : at + SLOT, cols] = rows[2 * SLOT : 3 * SLOT]
            side_ref[size + at : size + at + SLOT, cols] = rows[3 * SLOT :]


def pick(group, placing, blocks):
    tok, width = blocks[0].shape
    vmem = pl.BlockSpec(memory_space=pltpu.VMEM)
    rows = len(group) * SLOT
    return pl.pallas_call(
        functools.partial(pick_kernel, group),
        out_shape=[jax.ShapeDtypeStruct((k * rows, width), jnp.bfloat16) for k in (1, 1, 2)],
        in_specs=[vmem] + [pl.BlockSpec(memory_space=pltpu.HBM)] * len(blocks),
        out_specs=[vmem] * 3,
        scratch_shapes=[
            pltpu.VMEM((len(blocks), tok, width), jnp.bfloat16),
            pltpu.SemaphoreType.DMA((len(blocks),)),
        ],
        compiler_params=pltpu.CompilerParams(vmem_limit_bytes=60 * 2**20),
        cost_estimate=pl.CostEstimate(
            flops=2 * 4 * rows * HD * width, bytes_accessed=16 * rows * width, transcendentals=0
        ),
    )(placing, *blocks)


def expert_kernel(spans, place_ref, *refs):
    count = len(spans)
    x_refs, w_refs, out_refs = refs[:count], refs[count : -5 - count], refs[-5 - count : -5]
    w_vmem, x_all, acc_ref, hid_ref, sems = refs[-5:]
    pieces = len(w_refs)
    depth = w_refs[0].shape[0]
    copies = [
        pltpu.make_async_copy(w_refs[j], w_vmem.at[j], sems.at[j]) for j in range(pieces)
    ]
    for copy in copies:
        copy.start()
    for x_ref, (at, size) in zip(x_refs, spans):
        x_all[at : at + size] = x_ref[...]
    both = acc_ref.shape[1]
    ffe = both // 2
    hid_ref[...] = jnp.zeros_like(hid_ref)
    for j in range(pieces):
        copies[j].wait()
        cols = pl.ds(pl.multiple_of(place_ref[j] * depth, depth), depth)
        part = jnp.dot(x_all[:, cols], w_vmem[j, :, :both], preferred_element_type=jnp.float32)
        if j == 0:
            acc_ref[...] = part
        else:
            acc_ref[...] += part
    gate = acc_ref[:, :ffe]
    up = acc_ref[:, ffe:]
    hid_ref[:, :ffe] = (gate / (1.0 + jnp.exp(-gate)) * up).astype(jnp.bfloat16)
    hid = hid_ref[...]
    for j in range(pieces):
        cols = pl.ds(pl.multiple_of(place_ref[j] * depth, depth), depth)
        made = lax.dot_general(
            hid, w_vmem[j, :, both:], (((1,), (1,)), ((), ())), preferred_element_type=jnp.float32
        ).astype(jnp.bfloat16)
        for out_ref, (at, size) in zip(out_refs, spans):
            out_ref[:, cols] = made[at : at + size]


def expert(places, x, pieces, ffe):
    width = x[0].shape[1]
    depth, lanes = pieces[0].shape
    spans, total = [], 0
    for a in x:
        spans.append((total, a.shape[0]))
        total += a.shape[0]
    vmem = pl.BlockSpec(memory_space=pltpu.VMEM)
    return pl.pallas_call(
        functools.partial(expert_kernel, tuple(spans)),
        out_shape=[jax.ShapeDtypeStruct(a.shape, jnp.bfloat16) for a in x],
        in_specs=[pl.BlockSpec(memory_space=pltpu.SMEM)]
        + [vmem] * len(x)
        + [pl.BlockSpec(memory_space=pltpu.HBM)] * len(pieces),
        out_specs=[vmem] * len(x),
        scratch_shapes=[
            pltpu.VMEM((len(pieces), depth, lanes), jnp.bfloat16),
            pltpu.VMEM((total, width), jnp.bfloat16),
            pltpu.VMEM((total, 2 * ffe), jnp.float32),
            pltpu.VMEM((total, lanes - 2 * ffe), jnp.bfloat16),
            pltpu.SemaphoreType.DMA((len(pieces),)),
        ],
        compiler_params=pltpu.CompilerParams(vmem_limit_bytes=60 * 2**20),
        cost_estimate=pl.CostEstimate(
            flops=6 * total * width * ffe,
            bytes_accessed=6 * width * ffe + 4 * total * width,
            transcendentals=total * ffe,
        ),
    )(places, *x, *pieces)


def body(
    layer_input,
    queries,
    keys,
    values,
    out_weight,
    norm_gain,
    route_ids,
    route_weight,
    w_gate,
    w_up,
    w_down,
):
    tok = layer_input.shape[1]
    ctx = lax.axis_index("ctx")
    exp = lax.axis_index("exp")
    core, y, xh = ctx % 2, ctx // 2 % NY, ctx // (2 * NY)
    z, xl = exp // 2, exp % 2
    same_core = [[p * 2 + c for p in range(2 * NY)] for c in range(2)]

    ffe = w_gate.shape[2]
    lanes = -(-3 * ffe // HD) * HD
    down_rows = jnp.swapaxes(w_down, 1, 2)
    blank = jnp.zeros((w_gate.shape[1], lanes - 3 * ffe), w_gate.dtype)

    def local(e):
        return jnp.concatenate([w_gate[e], w_up[e], down_rows[e], blank], axis=1)

    first = core == 0
    zero, one = local(0), local(1)
    come = ctx_shift(jnp.where(first, one, zero), 0, 0, 1)
    piece = jnp.concatenate(
        [jnp.where(first, zero, come), jnp.where(first, come, one)], axis=0
    )
    far = ctx_shift(piece, 1, 0, 0)
    near_up, near_down = ctx_shift(piece, 0, 1, 0), ctx_shift(piece, 0, -1, 0)

    picks = jnp.concatenate([route_ids[0].T.astype(jnp.float32), route_weight[0].T], axis=0)
    picks = picks[None]
    picks = jnp.concatenate([picks, z_shift(picks, 1)], axis=0)

    heads = jnp.stack([queries[0], keys[0], values[0]]).reshape(3, tok, -1, HD)
    heads = heads.transpose(2, 0, 1, 3)
    own = lax.all_to_all(heads, "ctx", 0, 0, axis_index_groups=same_core, tiled=True)
    own, picks = lax.optimization_barrier((own, picks))
    other = ctx_shift(own, 0, 0, 1)
    picks = jnp.concatenate([picks, z_shift(picks, 2)], axis=0)
    attended = attend(core.reshape(1), own, other)
    attended, picks = lax.optimization_barrier((attended, picks))
    picks = jnp.concatenate([picks, z_shift(picks, 4)], axis=0)
    attended = lax.all_to_all(attended, "ctx", 0, 0, axis_index_groups=same_core, tiled=True)
    attended, picks, far, near_up, near_down = lax.optimization_barrier(
        (attended, picks, far, near_up, near_down)
    )
    near_two, far_down = ctx_shift(near_up, 0, 1, 0), ctx_shift(far, 0, -1, 0)

    top = route_ids.shape[2]
    ids, weights = picks[:, :top], picks[:, top:]
    quarter = jnp.arange(4)
    wanted = (4 * z + ((2 * xl + core) ^ quarter)).astype(jnp.float32)
    hits = ids[:, None] == wanted[None, :, None, None]
    hit = jnp.sum(hits.astype(jnp.float32), axis=2)
    share = jnp.sum(jnp.where(hits, weights[:, None], 0.0), axis=2)
    before = (jnp.arange(tok)[:, None] < jnp.arange(tok)[None, :]).astype(jnp.bfloat16)
    rank = jnp.einsum(
        "drs,st->drt", hit.astype(jnp.bfloat16), before, preferred_element_type=jnp.float32
    )
    slots = jnp.arange(SLOT, dtype=jnp.float32)
    at_slot = rank[:, :, None, :] == slots[None, None, :, None]
    placing = jnp.where(at_slot, hit[:, :, None, :], 0.0).reshape(NZ, 4 * SLOT, tok)
    placing = placing.astype(jnp.bfloat16)
    merging = jnp.where(at_slot, share[:, :, None, :], 0.0).reshape(NZ, 4 * SLOT, tok)
    merging = merging.transpose(0, 2, 1).astype(jnp.bfloat16)

    residual, normed = project(attended, out_weight, layer_input[0], norm_gain[None])

    swaps = (lambda a: a, lambda a: ctx_shift(a, 0, 0, 1), x_swap, diag_swap)

    half = tok // 2
    blocks = {0: normed}
    for d in (1, 2, 3):
        blocks[d] = z_shift(blocks[d - 1], 1)
        blocks[NZ - d] = z_shift(blocks[(NZ - d + 1) % NZ], -1)
    blocks[4] = jnp.concatenate(
        [z_shift(blocks[3][:half], 1), z_shift(blocks[5][half:], -1)], axis=0
    )
    inputs = [[blocks[d] for d in group] for group in GROUPS]
    sizes = [len(group) * SLOT for group in GROUPS]
    own, cross, side = {}, {}, {}

    def send(g):
        own[g], cross[g], leaving = pick(GROUPS[g], placing, inputs[g])
        side[g] = x_swap(leaving)

    def over_cores(groups, a, b):
        both = swaps[1](jnp.concatenate([a[g] for g in groups] + [b[g] for g in groups], axis=0))
        out, at = [], 0
        for _ in range(2):
            parts = {}
            for g in groups:
                parts[g] = both[at : at + sizes[g]]
                at += sizes[g]
            out.append(parts)
        return out

    inputs[0], near_two, far_down = lax.optimization_barrier((inputs[0], near_two, far_down))
    far_up, far_two = ctx_shift(far, 0, 1, 0), ctx_shift(far_down, 0, -1, 0)
    send(0)
    inputs[1], side[0], far_up, far_two = lax.optimization_barrier(
        (inputs[1], side[0], far_up, far_two)
    )
    send(1)
    picked = pick(GROUPS[2], placing, inputs[2])
    inputs[3], side[1], picked = lax.optimization_barrier((inputs[3], side[1], picked))
    spots = ((0, 0), (1, 0), (0, -1), (0, 1), (1, -1), (1, 1), (0, 2), (1, 2))
    pieces = [piece, far, near_up, near_down, far_up, far_down, near_two, far_two]
    places = jnp.stack([(xh + dx) % 2 * NY + (y + dy) % NY for dx, dy in spots])

    def halves_of(g):
        return side[g][: sizes[g]], side[g][sizes[g] :]

    straight, slant = {}, {}
    for g in (0, 1):
        straight[g], slant[g] = halves_of(g)
    core_rows, far_rows = over_cores((0, 1), cross, slant)

    def send_straight(g, rows):
        return [rows[0], swaps[1](rows[1]), x_swap(rows[2][: sizes[g]]), diag_swap(rows[2][sizes[g] :])]

    middle = send_straight(2, picked)
    last = pick(GROUPS[3], placing, inputs[3])
    core_rows, last = lax.optimization_barrier((core_rows, last))
    final = send_straight(3, last)
    early = expert(
        places,
        [kind[g] for kind in (own, straight, core_rows, far_rows) for g in (0, 1)],
        pieces,
        ffe,
    )
    early, middle, final = lax.optimization_barrier((early, middle, final))

    def send_back(rows):
        own_rows, beside, core_rows, far_rows = rows
        return [own_rows, swaps[1](core_rows), x_swap(beside), diag_swap(far_rows)]

    final = expert(places, final, pieces, ffe)
    final = [swaps[r](final[r]) for r in range(4)]
    middle = expert(places, middle, pieces, ffe)
    final, middle = lax.optimization_barrier((final, middle))
    done = {3: final, 2: [swaps[r](middle[r]) for r in range(4)]}
    done |= {1: send_back(early[1::2]), 0: send_back(early[0::2])}

    def returned(d):
        g = next(i for i, group in enumerate(GROUPS) if d in group)
        i = GROUPS[g].index(d)
        return jnp.concatenate([a[i * SLOT : (i + 1) * SLOT] for a in done[g]], axis=0)

    def part(d, h):
        return jnp.dot(
            merging[d, h * half : (h + 1) * half], returned(d), preferred_element_type=jnp.float32
        )

    def narrow(a):
        return a.astype(jnp.bfloat16)

    def wide(a):
        return a.astype(jnp.float32)

    up = [z_shift(narrow(part(4, 0)), 1), None]
    down = [None, z_shift(narrow(part(4, 1)), -1)]
    up, down, done[2], done[1] = lax.optimization_barrier((up, down, done[2], done[1]))
    for d in (3, 2, 1):
        for h in range(2):
            more = part(NZ - d, h)
            up[h] = z_shift(narrow(more if up[h] is None else more + wide(up[h])), 1)
            more = part(d, 1 - h)
            kept = down[1 - h]
            down[1 - h] = z_shift(narrow(more if kept is None else more + wide(kept)), -1)
        if d == 3:
            up, down, done[0] = lax.optimization_barrier((up, down, done[0]))
    mixed = [
        narrow(wide(residual[h * half : (h + 1) * half]) + part(0, h) + wide(up[h]) + wide(down[h]))
        for h in range(2)
    ]
    return jnp.concatenate(mixed, axis=0)[None]


def solution(mesh):
    return jax.shard_map(
        body,
        mesh=mesh,
        in_specs=(
            P("exp", "ctx", None),
            P("exp", "ctx", None),
            P("exp", "ctx", None),
            P("exp", "ctx", None),
            P(),
            P(),
            P("exp", "ctx", None),
            P("exp", "ctx", None),
            P("exp", "ctx", None),
            P("exp", "ctx", None),
            P("exp", None, "ctx"),
        ),
        out_specs=P("exp", "ctx", None),
        check_vma=False,
    )
```
